128 devices in a mesh: band: 16 (over x_lo, y, core), space: 8 (over z, x_hi).
Axes of the slice: x: 4 (x_hi: 2, x_lo: 2; x = x_hi * 2 + x_lo), y: 4, z: 4, core: 2. Of those that a mesh axis runs over, the one named last changes fastest.
Arguments:
- orbitals: bfloat16 [16, 192, 192, 192], P('band', 'space'), may hold values from -4 to 4
- occupations: float32 [16], P('band'), may hold values from 0.25 to 1
- shifts: float32 [16], P('band'), may hold values from 0.25 to 2
- perturbations: float32 [1, 192, 192, 192], P(None, 'space'), may hold values from -3 to 3
- local_potential: float32 [192, 192, 192], P('space'), may hold values from 0 to 1
Outputs:
- response_potential: float32 [1, 192, 192, 192], P(None, 'space', 'band')
The draws below stay inside these ranges and needn't reach their ends.
All inputs are finite; a program needn't handle non-finite values.
Results may differ from the reference program's by a relative error of at most 0.0003.
Values sent between devices are 32-bit elements; how exact they have to be, the bound alone decides.
A program may use at most 256 MiB of HBM per device.

```python
import math
import jax
import jax.numpy as jnp
from jax import lax

NG = 192
PERT = 1
APPLY = 2
ORBS = 16


def draw_perturbations(key, part):
    field = 0.5 * jax.random.normal(key, (PERT, NG, NG, NG), jnp.float32)
    return jnp.clip(field, -3.0, 3.0)


def block_levels(key, dims, split, least, largest):
    gain = 1.0
    for position, parts in split:
        draws = jax.random.uniform(jax.random.fold_in(jax.random.fold_in(key, 6), position), (parts,), jnp.float32, least / len(split), largest / len(split))
        gain = gain * jnp.repeat(jnp.exp(draws), dims[position] // parts).reshape((-1,) + (1,) * (len(dims) - 1 - position))
    return gain


def bell_draw(stream_key, extent, width, bound, split=(), kind=jnp.bfloat16):
    level = block_levels(stream_key, extent, split, -0.22, 0.18) if split else 1.0
    drawn = jax.random.normal(stream_key, extent, jnp.float32) * width * level
    return jnp.minimum(jnp.maximum(drawn, -bound), bound).astype(kind)


def setup_inputs(seed: int = 0) -> dict:
    splits = jax.random.split(jax.random.key(seed), 6)
    return {
        "orbitals": bell_draw(splits[0], (ORBS, NG, NG, NG), 1.0, 4.0, ((0, 16), (1, 8))),
        "occupations": jnp.clip(jnp.exp(math.log(1.0) - 1.3862944 * jax.random.uniform(splits[1], (ORBS,), jnp.float32) ** block_levels(splits[1], (ORBS,), ((0, 16),), -0.2, 0.2)), 0.25, 1.0),
        "shifts": jnp.clip(jnp.exp(math.log(2.0) - 2.0794415 * jax.random.uniform(splits[2], (ORBS,), jnp.float32) ** block_levels(splits[2], (ORBS,), ((0, 16),), -0.2, 0.2)), 0.25, 2.0),
        "perturbations": draw_perturbations(jax.random.fold_in(splits[5], 71), 0),
        "local_potential": jnp.clip(1.0 * jax.random.uniform(splits[4], (NG, NG, NG), jnp.float32) ** block_levels(splits[4], (NG, NG, NG), ((0, 8),), -0.2, 0.2), 0.0, 1.0),
    }


COEFFS = (-205.0 / 72.0, 8.0 / 5.0, -1.0 / 5.0, 8.0 / 315.0, -1.0 / 560.0)

def laplacian(field):
    total = 3.0 * COEFFS[0] * field
    for offset in range(1, 5):
        for along in (1, 2, 3):
            total = total + COEFFS[offset] * (jnp.roll(field, offset, along) + jnp.roll(field, -offset, along))
    return total

def reference(orbitals, occupations, shifts, perturbations, local_potential):
    count = orbitals.shape[0]

    def accumulate(index, density):
        wave = orbitals[index].astype(jnp.float32)[None]
        shift_value = shifts[index]
        potential_plus = local_potential[None] + shift_value
        centre = shift_value + 5.5
        ratio_c = centre / 5.5
        source = -(perturbations * wave)
        iterate = jnp.zeros_like(source)
        residual = source
        direction = source / centre
        weight = 1.0 / ratio_c
        for repeat in range(APPLY):
            iterate = iterate + direction
            image = -0.5 * laplacian(direction) + potential_plus * direction
            residual = residual - image
            weight_new = 1.0 / (2.0 * ratio_c - weight)
            direction = weight_new * weight * direction + 2.0 * weight_new / 5.5 * residual
            weight = weight_new
        solved = iterate + direction
        return density + occupations[index] * wave * solved
    density = lax.fori_loop(0, count, accumulate, jnp.zeros(perturbations.shape, jnp.float32))
    density = density * (4.0 / count)
    freq = jnp.arange(NG, dtype=jnp.int32)
    folded_k = jnp.minimum(freq, NG - freq).astype(jnp.float32)
    squares = folded_k * folded_k
    kernel = 256.0 / jnp.sqrt(squares[:, None, None] + squares[None, :, None] + squares[None, None, :] + 1.0)
    spectrum = jnp.fft.fftn(density, axes=(1, 2, 3))
    return jnp.real(jnp.fft.ifftn(spectrum * kernel, axes=(1, 2, 3))).astype(jnp.float32)
```

```python
import functools
import math

import jax
import jax.numpy as jnp
import numpy as np
from jax import lax
from jax.experimental import pallas as pl
from jax.experimental.pallas import tpu as pltpu
from jax.sharding import PartitionSpec as P

MESH = pl.DeviceIdType.MESH
BF16 = jnp.bfloat16
F32 = jnp.float32
NG = 192
SLAB = 24
EXT = 32
COEFFS = (-205.0 / 72.0, 8.0 / 5.0, -1.0 / 5.0, 8.0 / 315.0, -1.0 / 560.0)
WEIGHTS = (8064.0, -1008.0, 128.0, -9.0)
ROWS = 288
PIECE = 4 * ROWS // 8


def cas(product):
    angles = (np.asarray(product, np.int64) % NG).astype(np.float64) * (2.0 * math.pi / NG)
    return np.cos(angles) + np.sin(angles)


def halves(table):
    table = np.asarray(table, np.float32)
    high = table.astype(jnp.bfloat16)
    low = (table - high.astype(np.float32)).astype(jnp.bfloat16)
    return np.stack([high, low])


def tables():
    index = np.arange(NG)
    plain = cas(index[:, None] * index[None, :])
    stencil = np.zeros((NG, NG), np.float32)
    for offset, weight in enumerate(WEIGHTS, 1):
        for sign in (1, -1):
            stencil[index, (index + sign * offset) % NG] += weight
    forward_z = halves(plain).reshape(2 * NG, NG)
    forward_y = np.zeros((2, 256, 256))
    for layer in range(2):
        forward_y[layer, :128, :NG] = plain[:128]
        forward_y[layer, 128 + 64 * layer : 192 + 64 * layer, :NG] = plain[128:]
    forward_x = np.zeros((NG, 256))
    for core in range(2):
        for space in range(8):
            for slot in range(16):
                step, layer = divmod(slot, 2)
                ext = (14 - 2 * step if core == 0 else 16 + 2 * step) + layer
                x = (SLAB * space + ext - 4) % NG
                forward_x[:, (core * 8 + space) * 16 + slot] = plain[:, x]
    inverse_y = np.zeros((256, 256))
    inverse_z = np.zeros((256, NG))
    for band in range(16):
        inverse_y[band * 16 : band * 16 + 12, :NG] = plain[band * 12 : band * 12 + 12]
        x_lo, y, core = band // 8, (band // 2) % 4, band % 2
        first = 24 * (2 * y + x_lo) + 12 * core
        inverse_z[band * 16 : band * 16 + 12] = plain[first : first + 12]
    return (
        stencil.astype(jnp.bfloat16),
        forward_z,
        halves(forward_y),
        halves(forward_x),
        halves(plain),
        halves(inverse_y),
        halves(inverse_z),
    )


def split(value):
    high = value.astype(BF16)
    low = (value - high.astype(F32)).astype(BF16)
    return high, low


def dot(a, b, dims=((1,), (0,))):
    return lax.dot_general(a, b, (dims, ((), ())), preferred_element_type=F32)


def dot3_table_left(table, value, dims=((1,), (0,))):
    high, low = split(value)
    return dot(table[0], high, dims) + (dot(table[1], high, dims) + dot(table[0], low, dims))


def dot3_table_right(value, table):
    high, low = split(value)
    return dot(high, table[0]) + (dot(low, table[0]) + dot(high, table[1]))


def pack_into(ref, index, layer):
    ref[index, :NG, :] = layer[:, :128]
    ref[index, NG:, :64] = layer[:96, 128:]
    ref[index, NG:, 64:] = layer[96:, 128:]


def unpacked(ref, row):
    main = ref[pl.ds(row, NG), :]
    tail = ref[pl.ds(row + NG, 96), :]
    return main, tail


def kernel(
    coef, orb_hbm, pert_hbm, pot_hbm, stencil, tab_z, tab_fy, tab_fx, tab_p, tab_iy, tab_iz, out,
    orb, pert, pot, v, e,
    osend, orecv, psend, precv, pout,
    mine, other, crecv, yrecv, xsum, xrecv, red,
    gsend, grecv, wsend, wrecv, brow, zsend, zrecv, mat,
    load_sem, osem, psem, fsem, csem, ysem, xsem, gsem, wsem, zsem,
):
    band = lax.axis_index("band")
    space = lax.axis_index("space")
    core = lax.rem(band, 2)
    y = lax.rem(band // 2, 4)
    x_lo = band // 8
    group = 2 * y + x_lo
    up = lax.rem(space + 1, 8)
    down = lax.rem(space + 7, 8)

    def band_of(x, yy, c):
        return x * 8 + yy * 2 + c

    def y_at(k):
        return lax.rem(y + k, 4)

    loads = []
    for number, (src, dst, lead, lo, hi) in enumerate(
        (
            (pert_hbm, pert, True, 0, 4),
            (pert_hbm, pert, True, 20, 24),
            (orb_hbm, orb, True, 0, 4),
            (orb_hbm, orb, True, 20, 24),
            (orb_hbm, orb, True, 4, 20),
            (pert_hbm, pert, True, 4, 20),
            (pot_hbm, pot, False, 0, 24),
        )
    ):
        source = src.at[0, lo:hi] if lead else src.at[lo:hi]
        target = dst.at[4 + lo : 4 + hi] if dst is not pot else dst.at[lo:hi]
        copy = pltpu.make_async_copy(source, target, load_sem.at[number])
        copy.start()
        loads.append(copy)

    barrier = pltpu.get_barrier_semaphore()
    for k in range(1, 16):
        pl.semaphore_signal(
            barrier, inc=1, device_id=(lax.rem(band + k, 16), space), device_id_type=MESH
        )
    for k in range(1, 8):
        for c in range(2):
            pl.semaphore_signal(
                barrier,
                inc=1,
                device_id=(band_of(x_lo, y, c), lax.rem(space + k, 8)),
                device_id_type=MESH,
            )

    for layer in list(range(0, 8)) + list(range(32, 40)):
        e[layer] = jnp.zeros((NG, NG), F32)

    piece = 2 * y + core
    piece_row = pl.multiple_of(piece * PIECE, 8)
    half_row = pl.multiple_of(lax.rem(piece, 2) * PIECE, 8)
    loads[0].wait()
    loads[1].wait()
    pack_into(psend, 0, pert[24 + piece // 2])
    pack_into(psend, 1, pert[4 + piece // 2])
    loads[2].wait()
    loads[3].wait()

    pl.semaphore_wait(barrier, 29)

    pcopies, ocopies = [], {}
    for way, target in ((0, up), (1, down)):
        copy = pltpu.make_async_remote_copy(
            src_ref=psend.at[way, pl.ds(half_row, PIECE)],
            dst_ref=precv.at[way, pl.ds(piece_row, PIECE)],
            send_sem=psem.at[0, way],
            recv_sem=psem.at[1, way],
            device_id=(band, target),
            device_id_type=MESH,
        )
        copy.start()
        pcopies.append(copy)
    for near in range(4):
        for way, target in ((0, up), (1, down)):
            layer = 3 - near if way == 0 else near
            pack_into(
                osend.at[way], layer, orb[(24 if way == 0 else 4) + layer].astype(F32)
            )
            copy = pltpu.make_async_remote_copy(
                src_ref=osend.at[way, layer],
                dst_ref=orecv.at[way, layer],
                send_sem=osem.at[0, way, layer],
                recv_sem=osem.at[1, way, layer],
                device_id=(band, target),
                device_id_type=MESH,
            )
            copy.start()
            ocopies[way, layer] = copy

    def forwards(way):
        copies = []
        for other_piece in range(1, 8):
            to = lax.rem(piece + other_piece, 8)
            copies.append(
                pltpu.make_async_remote_copy(
                    src_ref=precv.at[way, pl.ds(piece_row, PIECE)],
                    dst_ref=precv.at[way, pl.ds(piece_row, PIECE)],
                    send_sem=fsem.at[0, way, other_piece],
                    recv_sem=fsem.at[1, way, other_piece],
                    device_id=(band_of(x_lo, to // 2, lax.rem(to, 2)), space),
                    device_id_type=MESH,
                )
            )
        return copies

    a_own, b_own, b_sten, q_shift = coef[0], coef[1], coef[2], coef[3]
    g0, g1, beta, beta_sten, factor = coef[4], coef[5], coef[6], coef[7], coef[8]

    loads[4].wait()
    loads[5].wait()
    loads[6].wait()

    def make_v(layer, carry):
        v[layer] = orb[layer].astype(F32) * pert[layer]
        return carry

    lax.fori_loop(4, 28, make_v, 0)

    def shifted(ref, layer):
        value = ref[layer]
        high, low = split(value)
        total = WEIGHTS[0] * (ref[layer - 1] + ref[layer + 1])
        for offset in range(2, 5):
            total += WEIGHTS[offset - 1] * (ref[layer - offset] + ref[layer + offset])
        total += dot(high, stencil[...]) + dot(low, stencil[...])
        total += dot(stencil[...], high) + dot(stencil[...], low)
        return value, total

    def make_e(layer, carry):
        value, total = shifted(v, layer + 4)
        diagonal = pot[layer] + q_shift
        e[layer + 8] = (a_own - b_own * diagonal) * value + b_sten * total
        return carry

    def transformed(layer):
        value, total = shifted(e, layer + 4)
        own = jnp.logical_and(layer >= 4, layer < 28)
        diagonal = pot[jnp.clip(layer - 4, 0, SLAB - 1)] + q_shift
        base = jnp.where(own, g0, 0.0)
        solved = base * v[layer] + (g1 - beta * diagonal) * value + beta_sten * total
        density = factor * orb[layer].astype(F32) * solved
        high, low = split(density)
        last = ((1,), (1,))
        both = dot(tab_z[...], high, last)
        return both[:NG] + (both[NG:] + dot(tab_z[:NG], low, last))

    def make_pair(ref, index, base):
        first = transformed(base)
        ref[index, 0] = first[:, :128]
        ref[index, 2, :, :64] = first[:, 128:]
        second = transformed(base + 1)
        ref[index, 1] = second[:, :128]
        ref[index, 2, :, 64:] = second[:, 128:]

    def base_of(c, j):
        return jnp.where(c == 0, 14 - 2 * j, 16 + 2 * j)

    def core_copy(j):
        return pltpu.make_async_remote_copy(
            src_ref=other.at[j],
            dst_ref=crecv.at[j],
            send_sem=csem.at[0, j],
            recv_sem=csem.at[1, j],
            device_id=(band_of(x_lo, y, 1 - core), space),
            device_id_type=MESH,
        )

    def y_copy(j, k):
        row = pl.multiple_of(48 * y_at(k), 8)
        return pltpu.make_async_remote_copy(
            src_ref=mine.at[j, :, pl.ds(row, 48)],
            dst_ref=yrecv.at[k - 1, j],
            send_sem=ysem.at[0, k - 1, j],
            recv_sem=ysem.at[1, k - 1, j],
            device_id=(band_of(x_lo, y_at(k), core), space),
            device_id_type=MESH,
        )

    def x_copy(j):
        row = pl.multiple_of(24 * (1 - x_lo), 8)
        return pltpu.make_async_remote_copy(
            src_ref=xsum.at[j, :, pl.ds(row, 24)],
            dst_ref=xrecv.at[j],
            send_sem=xsem.at[0, j],
            recv_sem=xsem.at[1, j],
            device_id=(band_of(1 - x_lo, y, core), space),
            device_id_type=MESH,
        )

    def compute_step(j):
        make_pair(other, j, base_of(1 - core, j))
        core_copy(j).start()
        make_pair(mine, j, base_of(core, j))

    def reduce_core(j):
        core_copy(j).wait_recv()
        mine[j] += crecv[j]
        for k in (2, 1, 3):
            y_copy(j, k).start()

    def reduce_y(j):
        for k in (1, 2, 3):
            y_copy(j, k).wait_recv()
        row = pl.multiple_of(48 * y, 8)
        xsum[j] = (mine[j, :, pl.ds(row, 48)] + yrecv[0, j]) + (yrecv[1, j] + yrecv[2, j])
        x_copy(j).start()

    def reduce_x(j):
        x_copy(j).wait_recv()
        row = pl.multiple_of(24 * x_lo, 8)
        red[j] = xsum[j, :, pl.ds(row, 24)] + xrecv[j]

    def step(j, carry):
        @pl.when(j < 8)
        def _():
            compute_step(j)

        @pl.when(jnp.logical_and(j >= 1, j < 9))
        def _():
            reduce_core(j - 1)

        @pl.when(jnp.logical_and(j >= 3, j < 11))
        def _():
            reduce_y(j - 3)

        @pl.when(j >= 4)
        def _():
            reduce_x(j - 4)

        return carry

    forward = {}
    for way in range(2):
        pcopies[way].wait_recv()
        forward[way] = forwards(way)
        for copy in forward[way]:
            copy.start()

    lax.fori_loop(4, 20, make_e, 0)
    lax.fori_loop(0, 2, step, 0)

    for way in range(2):
        for copy in forward[way]:
            copy.wait_recv()
        for layer in range(4):
            ocopies[way, layer].wait_recv()
            at = layer + (0 if way == 0 else 28)
            main, tail = unpacked(orecv.at[way, layer], 0)
            pmain, ptail = unpacked(precv.at[way], layer * ROWS)
            orb[at, :, :128] = main.astype(BF16)
            orb[at, :96, 128:] = tail[:, :64].astype(BF16)
            orb[at, 96:, 128:] = tail[:, 64:].astype(BF16)
            main = main * pmain
            tail = tail * ptail
            v[at, :, :128] = main
            v[at, :96, 128:] = tail[:, :64]
            v[at, 96:, 128:] = tail[:, 64:]

    lax.fori_loop(0, 4, make_e, 0)
    lax.fori_loop(20, 24, make_e, 0)
    lax.fori_loop(2, 12, step, 0)

    red0 = jnp.concatenate([red[:, 0].reshape(NG, 128), red[:, 2].reshape(NG, 128)], axis=1)
    red1 = jnp.concatenate([red[:, 1].reshape(NG, 128), red[:, 2].reshape(NG, 128)], axis=1)
    for layer, value in enumerate((red0, red1)):
        high, low = split(value)
        table_high, table_low = tab_fy[0, layer], tab_fy[1, layer]
        columns = dot(high, table_high) + (dot(low, table_high) + dot(high, table_low))
        for j in range(8):
            for half in range(2):
                gsend[pl.ds(half * 16 + 2 * j + layer, 24, stride=32), :] = columns[
                    24 * j : 24 * j + 24, 128 * half : 128 * half + 128
                ]

    mine_at = core * 8 + space

    def g_copy(k, c):
        to_space = lax.rem(space + k, 8)
        to_core = lax.rem(core + c, 2)
        row = pl.multiple_of(48 * (to_core * 8 + to_space), 8)
        return pltpu.make_async_remote_copy(
            src_ref=gsend.at[pl.ds(row, 48)],
            dst_ref=grecv.at[mine_at],
            send_sem=gsem.at[0, k, c],
            recv_sem=gsem.at[1, k, c],
            device_id=(band_of(x_lo, y, to_core), to_space),
            device_id_type=MESH,
        )

    partners = [(k, c) for k in (4, 3, 5, 2, 6, 1, 7, 0) for c in range(2) if (k, c) != (0, 0)]
    for k, c in partners:
        g_copy(k, c).start()
    grecv[mine_at] = gsend[pl.ds(pl.multiple_of(48 * mine_at, 8), 48), :]

    kx = lax.broadcasted_iota(jnp.int32, (NG, 128), 0)
    lane = lax.broadcasted_iota(jnp.int32, (NG, 128), 1)
    gx = jnp.minimum(kx, NG - kx)
    factors = []
    for unit in range(3):
        number = 3 * mine_at + unit
        kz = 24 * group + number // 2
        gz = jnp.minimum(kz, NG - kz)
        ky = lane + 128 * lax.rem(number, 2)
        gy = jnp.minimum(ky, NG - ky)
        square = (gx * gx + gy * gy + (gz * gz + 1)).astype(F32)
        factors.append((256.0 / float(NG) ** 3) / jnp.sqrt(square))
    coulomb = jnp.concatenate(factors, axis=1)

    for k, c in partners:
        g_copy(k, c).wait_recv()
    pencil = jnp.concatenate(
        [grecv[:, 16 * unit : 16 * unit + 16, :].reshape(256, 128) for unit in range(3)], axis=1
    )
    spectral = dot3_table_left(tab_fx, pencil) * coulomb
    restored = dot3_table_left(tab_p, spectral)
    for unit in range(3):
        wsend[unit] = restored[:, 128 * unit : 128 * unit + 128]

    def w_copy(k):
        to_space = lax.rem(space + k, 8)
        row = pl.multiple_of(24 * to_space, 8)
        return pltpu.make_async_remote_copy(
            src_ref=wsend.at[:, pl.ds(row, 24)],
            dst_ref=wrecv.at[pl.ds(3 * space, 3)],
            send_sem=wsem.at[0, k],
            recv_sem=wsem.at[1, k],
            device_id=(band, to_space),
            device_id_type=MESH,
        )

    for k in (4, 3, 5, 2, 6, 1, 7):
        w_copy(k).start()
    wrecv[pl.ds(3 * space, 3)] = wsend[:, pl.ds(pl.multiple_of(24 * space, 8), 24), :]
    brow[...] = jnp.zeros(brow.shape, F32)
    for k in (4, 3, 5, 2, 6, 1, 7):
        w_copy(k).wait_recv()

    for unit in range(24):
        brow[unit % 2, pl.ds(unit // 2, 24, stride=16), :] = wrecv[unit]
    rows = jnp.concatenate([brow[0], brow[1]], axis=1)
    zsend[...] = dot3_table_left(tab_iy, rows, ((1,), (1,)))

    def z_copy(k):
        to = lax.rem(band + k, 16)
        return pltpu.make_async_remote_copy(
            src_ref=zsend.at[pl.ds(pl.multiple_of(16 * to, 8), 16)],
            dst_ref=zrecv.at[band],
            send_sem=zsem.at[0, k],
            recv_sem=zsem.at[1, k],
            device_id=(to, space),
            device_id_type=MESH,
        )

    order = (4, 12, 8, 3, 5, 11, 13, 2, 6, 10, 14, 7, 9, 1, 15)
    for k in order:
        z_copy(k).start()
    zrecv[band] = zsend[pl.ds(pl.multiple_of(16 * band, 8), 16), :]
    for k in order:
        z_copy(k).wait_recv()

    granule = lax.broadcasted_iota(jnp.int32, (16, 128), 1) // 16
    for third in range(3):
        for part in range(2):
            blocks = [zrecv[8 * part + i, :, 128 * third : 128 * third + 128] for i in range(8)]
            for bit in (1, 2, 4):
                upper = lax.rem(granule // bit, 2) == 1
                after = list(blocks)
                for i in range(8):
                    if not i & bit:
                        low, high = blocks[i], blocks[i | bit]
                        after[i] = jnp.where(upper, pltpu.roll(high, 16 * bit, 1), low)
                        after[i | bit] = jnp.where(upper, high, pltpu.roll(low, 128 - 16 * bit, 1))
                blocks = after
            for i in range(8):
                x = 8 * third + i
                mat[16 * x : 16 * x + 16, 128 * part : 128 * part + 128] = blocks[i]
    result = dot3_table_right(mat[...], tab_iz)
    for x in range(SLAB):
        out[0, x] = result[16 * x : 16 * x + 12]

    for way in range(2):
        pcopies[way].wait_send()
        for copy in forward[way]:
            copy.wait_send()
        for layer in range(4):
            ocopies[way, layer].wait_send()

    def drain(j, carry):
        core_copy(j).wait_send()
        for k in (1, 2, 3):
            y_copy(j, k).wait_send()
        x_copy(j).wait_send()
        return carry

    lax.fori_loop(0, 8, drain, 0)
    for k, c in partners:
        g_copy(k, c).wait_send()
    for k in (4, 3, 5, 2, 6, 1, 7):
        w_copy(k).wait_send()
    for k in order:
        z_copy(k).wait_send()


def scalars(occupations, shifts):
    delta = 5.5
    shift = shifts[0]
    theta = shift + 5.5
    ratio = theta / delta
    w0 = 1.0 / ratio
    w1 = 1.0 / (2.0 * ratio - w0)
    w2 = 1.0 / (2.0 * ratio - w1)
    alpha1, beta1 = w1 * w0, 2.0 * w1 / delta
    alpha2, beta2 = w2 * w1, 2.0 * w2 / delta
    a = alpha1 / theta + beta1
    b = beta1 / theta
    g0 = (1.0 - w2 * w0) / theta
    g1 = 1.0 + alpha2 + beta2 / beta1
    q_shift = shift - 1.5 * COEFFS[0]
    factor = -occupations[0] * (4.0 / 16.0)
    return jnp.stack([a, b, b / 10080.0, q_shift, g0, g1, beta2, beta2 / 10080.0, factor])


def on_device(orbitals, occupations, shifts, perturbations, local_potential):
    consts = tables()
    any_space = pl.BlockSpec(memory_space=pl.ANY)
    vmem = pl.BlockSpec(memory_space=pltpu.VMEM)
    dma = pltpu.SemaphoreType.DMA
    return pl.pallas_call(
        kernel,
        out_shape=jax.ShapeDtypeStruct((1, SLAB, 12, NG), F32),
        in_specs=[pl.BlockSpec(memory_space=pltpu.SMEM)] + [any_space] * 3 + [vmem] * 7,
        out_specs=vmem,
        scratch_shapes=[
            pltpu.VMEM((EXT, NG, NG), BF16),
            pltpu.VMEM((EXT, NG, NG), F32),
            pltpu.VMEM((SLAB, NG, NG), F32),
            pltpu.VMEM((EXT, NG, NG), F32),
            pltpu.VMEM((EXT + 8, NG, NG), F32),
            pltpu.VMEM((2, 4, ROWS, 128), F32),
            pltpu.VMEM((2, 4, ROWS, 128), F32),
            pltpu.VMEM((2, ROWS, 128), F32),
            pltpu.VMEM((2, 4 * ROWS, 128), F32),
            pltpu.VMEM((8, 128), F32),
            pltpu.VMEM((8, 3, NG, 128), F32),
            pltpu.VMEM((8, 3, NG, 128), F32),
            pltpu.VMEM((8, 3, NG, 128), F32),
            pltpu.VMEM((3, 8, 3, 48, 128), F32),
            pltpu.VMEM((8, 3, 48, 128), F32),
            pltpu.VMEM((8, 3, 24, 128), F32),
            pltpu.VMEM((8, 3, 24, 128), F32),
            pltpu.VMEM((768, 128), F32),
            pltpu.VMEM((16, 48, 128), F32),
            pltpu.VMEM((3, NG, 128), F32),
            pltpu.VMEM((24, 24, 128), F32),
            pltpu.VMEM((2, 384, 128), F32),
            pltpu.VMEM((256, 384), F32),
            pltpu.VMEM((16, 16, 384), F32),
            pltpu.VMEM((384, 256), F32),
            dma((7,)),
            dma((2, 2, 4)),
            dma((2, 2)),
            dma((2, 2, 8)),
            dma((2, 8)),
            dma((2, 3, 8)),
            dma((2, 8)),
            dma((2, 8, 2)),
            dma((2, 8)),
            dma((2, 16)),
        ],
        compiler_params=pltpu.CompilerParams(
            collective_id=0, has_side_effects=True, vmem_limit_bytes=60 * 2**20
        ),
        name="response",
    )(scalars(occupations, shifts), orbitals, perturbations, local_potential, *map(jnp.asarray, consts))


def solution(mesh):
    in_specs = (
        P("band", "space", None, None),
        P("band"),
        P("band"),
        P(None, "space", None, None),
        P("space", None, None),
    )
    out_specs = P(None, "space", "band", None)
    return jax.shard_map(
        on_device, mesh=mesh, in_specs=in_specs, out_specs=out_specs, check_vma=False
    )
```

```python
import math

import jax
import jax.numpy as jnp
import numpy as np
from jax import lax
from jax.experimental import pallas as pl
from jax.experimental.pallas import tpu as pltpu
from jax.sharding import PartitionSpec as P

MESH = pl.DeviceIdType.MESH
BF16 = jnp.bfloat16
F32 = jnp.float32
NG = 192
SLAB = 24
EXT = 32
COEFFS = (-205.0 / 72.0, 8.0 / 5.0, -1.0 / 5.0, 8.0 / 315.0, -1.0 / 560.0)
WEIGHTS = (8064.0, -1008.0, 128.0, -9.0)
ROWS = 288
PIECE = 4 * ROWS // 8


def cas(product):
    angles = (np.asarray(product, np.int64) % NG).astype(np.float64) * (2.0 * math.pi / NG)
    return np.cos(angles) + np.sin(angles)


def halves(table):
    table = np.asarray(table, np.float32)
    high = table.astype(jnp.bfloat16)
    low = (table - high.astype(np.float32)).astype(jnp.bfloat16)
    return np.stack([high, low])


def tables():
    index = np.arange(NG)
    plain = cas(index[:, None] * index[None, :])
    stencil = np.zeros((NG, NG), np.float32)
    for offset, weight in enumerate(WEIGHTS, 1):
        for sign in (1, -1):
            stencil[index, (index + sign * offset) % NG] += weight
    forward_y = np.zeros((2, 256, 256))
    for layer in range(2):
        forward_y[layer, :128, :NG] = plain[:128]
        forward_y[layer, 128 + 64 * layer : 192 + 64 * layer, :NG] = plain[128:]
    forward_x = np.zeros((NG, 256))
    for core in range(2):
        for space in range(8):
            for slot in range(16):
                step, layer = divmod(slot, 2)
                ext = (14 - 2 * step if core == 0 else 16 + 2 * step) + layer
                x = (SLAB * space + ext - 4) % NG
                forward_x[:, (core * 8 + space) * 16 + slot] = plain[:, x]
    inverse_y = np.zeros((256, 256))
    inverse_z = np.zeros((256, NG))
    for band in range(16):
        inverse_y[band * 16 : band * 16 + 12, :NG] = plain[band * 12 : band * 12 + 12]
        x_lo, y, core = band // 8, (band // 2) % 4, band % 2
        first = 24 * (2 * y + x_lo) + 12 * core
        inverse_z[band * 16 : band * 16 + 12] = plain[first : first + 12]
    pieces = {
        "stencil": stencil.astype(jnp.bfloat16)[None],
        "plain": halves(plain),
        "forward_y0": halves(forward_y[0]),
        "forward_y1": halves(forward_y[1]),
        "forward_x": halves(forward_x),
        "inverse_y": halves(inverse_y),
        "inverse_z": halves(inverse_z),
    }
    where, rows, start = {}, [], 0
    for name, piece in pieces.items():
        count, height, width = piece.shape
        where[name] = (start, count, height, width)
        flat = piece.reshape(count * height, width)
        rows.append(np.pad(flat, ((0, 0), (0, 256 - width))))
        start += count * height
    return where, np.concatenate(rows)


WHERE, TABLE = tables()


def split(value):
    high = value.astype(BF16)
    low = (value - high.astype(F32)).astype(BF16)
    return high, low


def dot(a, b, dims=((1,), (0,))):
    return lax.dot_general(a, b, (dims, ((), ())), preferred_element_type=F32)


def dot3_table_left(table, value, dims=((1,), (0,))):
    high, low = split(value)
    return dot(table[0], high, dims) + (dot(table[1], high, dims) + dot(table[0], low, dims))


def dot3_table_right(value, table):
    high, low = split(value)
    return dot(high, table[0]) + (dot(low, table[0]) + dot(high, table[1]))


def pack_into(ref, index, layer):
    ref[index, :NG, :] = layer[:, :128]
    ref[index, NG:, :64] = layer[:96, 128:]
    ref[index, NG:, 64:] = layer[96:, 128:]


def unpacked(ref, row):
    main = ref[pl.ds(row, NG), :]
    tail = ref[pl.ds(row + NG, 96), :]
    return main, tail


def kernel(
    occ_ref, shift_ref, orb_hbm, pert_hbm, pot_hbm, table_hbm, out,
    table, orb, pert, pot, v, e,
    osend, orecv, psend, precv,
    mine, other, crecv, tiles, ya_recv, xsum, xb_recv, xa_recv, ysum, yb_recv, red,
    gsend, grecv, wsend, wrecv, brow, zsend, zrecv, mat,
    load_sem, osem, psem, fsem, csem, ya_sem, xb_sem, xa_sem, yb_sem, gsem, wsem, zsem, sent,
):
    band = lax.axis_index("band")
    space = lax.axis_index("space")
    core = lax.rem(band, 2)
    y = lax.rem(band // 2, 4)
    x_lo = band // 8
    group = 2 * y + x_lo
    up = lax.rem(space + 1, 8)
    down = lax.rem(space + 7, 8)

    def band_of(x, yy, c):
        return x * 8 + yy * 2 + c

    def y_at(k):
        return lax.rem(y + k, 4)

    def part(name, number=0):
        start, _, height, width = WHERE[name]
        return table[start + number * height : start + (number + 1) * height, :width]

    def pair_of(name):
        return part(name, 0), part(name, 1)

    def wait_bytes(ref, sem):
        pltpu.make_async_copy(ref, ref, sem).wait()

    def send(src, dst, send_sem, recv_sem, to_band, to_space):
        pltpu.make_async_remote_copy(
            src_ref=src,
            dst_ref=dst,
            send_sem=send_sem,
            recv_sem=recv_sem,
            device_id=(to_band, to_space),
            device_id_type=MESH,
        ).start()

    loads = []
    for number, (source, target) in enumerate(
        (
            (pert_hbm.at[0, 0:4], pert.at[4:8]),
            (pert_hbm.at[0, 20:24], pert.at[24:28]),
            (orb_hbm.at[0, 0:4], orb.at[4:8]),
            (orb_hbm.at[0, 20:24], orb.at[24:28]),
            (orb_hbm.at[0, 4:20], orb.at[8:24]),
            (pert_hbm.at[0, 4:20], pert.at[8:24]),
            (pot_hbm, pot),
            (table_hbm, table),
        )
    ):
        copy = pltpu.make_async_copy(source, target, load_sem.at[number])
        copy.start()
        loads.append(copy)

    barrier = pltpu.get_barrier_semaphore()
    for k in range(1, 8):
        for c in range(2):
            pl.semaphore_signal(
                barrier,
                inc=1,
                device_id=(band_of(x_lo, y, c), lax.rem(space + k, 8)),
                device_id_type=MESH,
            )
    for k in range(1, 16):
        pl.semaphore_signal(
            barrier, inc=1, device_id=(lax.rem(band + k, 16), space), device_id_type=MESH
        )

    for layer in list(range(0, 8)) + list(range(32, 40)):
        e[layer] = jnp.zeros((NG, NG), F32)

    delta = 5.5
    shift = jnp.full((1, NG), shift_ref[0], F32)
    theta = shift + 5.5
    ratio = theta / delta
    w0 = 1.0 / ratio
    w1 = 1.0 / (2.0 * ratio - w0)
    w2 = 1.0 / (2.0 * ratio - w1)
    beta1, beta = 2.0 * w1 / delta, 2.0 * w2 / delta
    a_own = w1 * w0 / theta + beta1
    b_own = beta1 / theta
    b_sten = b_own / 10080.0
    q_shift = shift - 1.5 * COEFFS[0]
    g0 = (1.0 - w2 * w0) / theta
    g1 = 1.0 + w2 * w1 + beta / beta1
    beta_sten = beta / 10080.0
    factor = jnp.full((1, NG), occ_ref[0], F32) * (-4.0 / 16.0)

    piece = 4 * core + y
    piece_row = pl.multiple_of(piece * PIECE, 8)
    half_row = pl.multiple_of(lax.rem(piece, 2) * PIECE, 8)
    loads[0].wait()
    loads[1].wait()
    pack_into(psend, 0, pert[24 + piece // 2])
    pack_into(psend, 1, pert[4 + piece // 2])
    loads[2].wait()
    loads[3].wait()

    pl.semaphore_wait(barrier, 29)

    for way, target in ((0, up), (1, down)):
        send(
            psend.at[way, pl.ds(half_row, PIECE)],
            precv.at[way, pl.ds(piece_row, PIECE)],
            sent.at[0], psem.at[way], band, target,
        )
    for near in range(2):
        for way, target in ((0, up), (1, down)):
            first = 2 - 2 * near if way == 0 else 2 * near
            for layer in (first, first + 1):
                pack_into(
                    osend.at[way], layer, orb[(24 if way == 0 else 4) + layer].astype(F32)
                )
            send(
                osend.at[way, first : first + 2],
                orecv.at[way, first : first + 2],
                sent.at[1], osem.at[way, near], band, target,
            )

    loads[4].wait()
    loads[5].wait()

    def make_v(layer, carry):
        v[layer] = orb[layer].astype(F32) * pert[layer]
        return carry

    lax.fori_loop(4, 28, make_v, 0)
    loads[6].wait()
    loads[7].wait()

    def along_x(ref, layer):
        total = WEIGHTS[0] * (ref[layer - 1] + ref[layer + 1])
        for offset in range(2, 5):
            total += WEIGHTS[offset - 1] * (ref[layer - offset] + ref[layer + offset])
        return total

    def shifted(ref, layer):
        value = ref[layer]
        high, low = split(value)
        total = along_x(ref, layer)
        stencil = part("stencil")
        total += dot(high, stencil) + dot(low, stencil)
        total += dot(stencil, high) + dot(stencil, low)
        return value, total

    def make_e(layer, carry):
        value, total = shifted(v, layer + 4)
        diagonal = pot[layer] + q_shift
        e[layer + 8] = (a_own - b_own * diagonal) * value + b_sten * total
        return carry

    def density_own(layer):
        value, total = shifted(e, layer + 4)
        diagonal = pot[layer - 4] + q_shift
        solved = g0 * v[layer] + (g1 - beta * diagonal) * value + beta_sten * total
        return factor * orb[layer].astype(F32) * solved

    def density_beyond(layer):
        return factor * orb[layer].astype(F32) * (beta_sten * along_x(e, layer + 4))

    def base_of(c, j):
        return jnp.where(c == 0, 14 - 2 * j, 16 + 2 * j)

    def make_pairs(j, density):
        def fill(layer, carry):
            other[j, layer] = density(base_of(1 - core, j) + layer)
            return carry

        lax.fori_loop(0, 2, fill, 0)
        send(
            other.at[j], crecv.at[j], sent.at[2], csem.at[j], band_of(x_lo, y, 1 - core), space
        )

        def fill_mine(layer, carry):
            mine[j, layer] = density(base_of(core, j) + layer)
            return carry

        lax.fori_loop(0, 2, fill_mine, 0)

    def transformed(value):
        high, low = split(value)
        last = ((1,), (1,))
        table_high, table_low = pair_of("plain")
        rows = dot(table_high, high, last) + (
            dot(table_low, high, last) + dot(table_high, low, last)
        )
        return rows.reshape(4, 2, 24, NG)

    def add_cores(j):
        wait_bytes(crecv.at[j], csem.at[j])
        first = transformed(mine[j, 0] + crecv[j, 0])
        tiles[j, 0] = first[..., :128]
        tiles[j, 2, :, :, :, :64] = first[..., 128:]
        second = transformed(mine[j, 1] + crecv[j, 1])
        tiles[j, 1] = second[..., :128]
        tiles[j, 2, :, :, :, 64:] = second[..., 128:]

    def ya_start(j):
        add_cores(j)
        for k in (2, 1, 3):
            send(
                tiles.at[j, :, y_at(k)], ya_recv.at[j, k - 1],
                sent.at[3], ya_sem.at[j], band_of(x_lo, y_at(k), core), space,
            )

    def ya_end(j):
        wait_bytes(ya_recv.at[j], ya_sem.at[j])
        xsum[j] = (tiles[j, :, y] + ya_recv[j, 0]) + (ya_recv[j, 1] + ya_recv[j, 2])
        send(
            xsum.at[j, :, 1 - x_lo], xb_recv.at[j],
            sent.at[4], xb_sem.at[j], band_of(1 - x_lo, y, core), space,
        )

    def xb_end(j):
        wait_bytes(xb_recv.at[j], xb_sem.at[j])
        red[j] = xsum[j, :, x_lo] + xb_recv[j]

    def xa_start(j):
        add_cores(j)
        send(
            tiles.at[j, :, :, 1 - x_lo], xa_recv.at[j - 4],
            sent.at[5], xa_sem.at[j - 4], band_of(1 - x_lo, y, core), space,
        )

    def xa_end(j):
        wait_bytes(xa_recv.at[j - 4], xa_sem.at[j - 4])
        ysum[j - 4] = tiles[j, :, :, x_lo] + xa_recv[j - 4]
        for k in (2, 1, 3):
            send(
                ysum.at[j - 4, :, y_at(k)], yb_recv.at[j - 4, k - 1],
                sent.at[6], yb_sem.at[j - 4], band_of(x_lo, y_at(k), core), space,
            )

    def yb_end(j):
        wait_bytes(yb_recv.at[j - 4], yb_sem.at[j - 4])
        red[j] = (ysum[j - 4, :, y] + yb_recv[j - 4, 0]) + (
            yb_recv[j - 4, 1] + yb_recv[j - 4, 2]
        )

    def repeat(lo, hi, *steps):
        def body(j, carry):
            for one in steps:
                one(j)
            return carry

        lax.fori_loop(lo, hi, body, 0)

    lax.fori_loop(4, 12, make_e, 0)

    for way in range(2):
        wait_bytes(precv.at[way, :PIECE], psem.at[way])
    for way in range(2):
        for k in (2, 1, 3):
            send(
                precv.at[way, pl.ds(piece_row, PIECE)],
                precv.at[way, pl.ds(piece_row, PIECE)],
                sent.at[7], fsem.at[0], band_of(x_lo, y_at(k), core), space,
            )
    lax.fori_loop(12, 20, make_e, 0)
    repeat(0, 1, lambda j: make_pairs(j, density_own))
    wait_bytes(precv.at[0, : 6 * PIECE], fsem.at[0])
    core_row = pl.multiple_of(core * 4 * PIECE, 8)
    for way in range(2):
        send(
            precv.at[way, pl.ds(core_row, 4 * PIECE)],
            precv.at[way, pl.ds(core_row, 4 * PIECE)],
            sent.at[8], fsem.at[1], band_of(x_lo, y, 1 - core), space,
        )
    repeat(1, 2, lambda j: make_pairs(j, density_own))
    repeat(0, 2, ya_start)

    def take_halo(near):
        for way in range(2):
            first = 2 - 2 * near if way == 0 else 2 * near
            wait_bytes(orecv.at[way, first : first + 2], osem.at[way, near])
            for layer in (first, first + 1):
                at = layer + (0 if way == 0 else 28)
                main, tail = unpacked(orecv.at[way, layer], 0)
                pmain, ptail = unpacked(precv.at[way], layer * ROWS)
                orb[at, :, :128] = main.astype(BF16)
                orb[at, :96, 128:] = tail[:, :64].astype(BF16)
                orb[at, 96:, 128:] = tail[:, 64:].astype(BF16)
                main = main * pmain
                tail = tail * ptail
                v[at, :, :128] = main
                v[at, :96, 128:] = tail[:, :64]
                v[at, 96:, 128:] = tail[:, 64:]
        repeat(2 - 2 * near, 4 - 2 * near, lambda j: make_e(j, 0))
        repeat(20 + 2 * near, 22 + 2 * near, lambda j: make_e(j, 0))

    wait_bytes(precv.at[0, : 8 * PIECE], fsem.at[1])
    take_halo(0)
    repeat(2, 3, lambda j: make_pairs(j, density_own), ya_start)
    repeat(0, 3, ya_end)
    take_halo(1)
    repeat(3, 5, lambda j: make_pairs(j, density_own))
    repeat(3, 4, ya_start)

    def tail(j):
        @pl.when(j < 5)
        def _():
            make_pairs(j + 1, density_own)

        @pl.when(jnp.logical_and(j >= 5, j < 7))
        def _():
            make_pairs(j + 1, density_beyond)

        xa_start(j)

        @pl.when(j >= 6)
        def _():
            xa_end(j - 2)

    repeat(4, 8, tail)
    repeat(3, 4, ya_end)
    repeat(6, 8, xa_end)
    repeat(0, 4, xb_end)
    repeat(4, 8, yb_end)

    red0 = jnp.concatenate([red[:, 0].reshape(NG, 128), red[:, 2].reshape(NG, 128)], axis=1)
    red1 = jnp.concatenate([red[:, 1].reshape(NG, 128), red[:, 2].reshape(NG, 128)], axis=1)
    for layer, value in enumerate((red0, red1)):
        high, low = split(value)
        table_high, table_low = pair_of("forward_y%d" % layer)
        columns = dot(high, table_high) + (dot(low, table_high) + dot(high, table_low))
        for j in range(8):
            for half in range(2):
                gsend[pl.ds(half * 16 + 2 * j + layer, 24, stride=32), :] = columns[
                    24 * j : 24 * j + 24, 128 * half : 128 * half + 128
                ]

    mine_at = core * 8 + space

    for k in (4, 3, 5, 2, 6, 1, 7, 0):
        for c in range(2):
            if (k, c) != (0, 0):
                to_space = lax.rem(space + k, 8)
                to_core = lax.rem(core + c, 2)
                row = pl.multiple_of(48 * (to_core * 8 + to_space), 8)
                send(
                    gsend.at[pl.ds(row, 48)], grecv.at[mine_at],
                    gsem.at[0], gsem.at[1], band_of(x_lo, y, to_core), to_space,
                )
    grecv[mine_at] = gsend[pl.ds(pl.multiple_of(48 * mine_at, 8), 48), :]

    kx = lax.broadcasted_iota(jnp.int32, (NG, 128), 0)
    lane = lax.broadcasted_iota(jnp.int32, (NG, 128), 1)
    gx = jnp.minimum(kx, NG - kx)
    factors = []
    for unit in range(3):
        number = 3 * mine_at + unit
        kz = 24 * group + number // 2
        gz = jnp.minimum(kz, NG - kz)
        ky = lane + 128 * lax.rem(number, 2)
        gy = jnp.minimum(ky, NG - ky)
        square = (gx * gx + gy * gy + (gz * gz + 1)).astype(F32)
        factors.append((256.0 / float(NG) ** 3) / jnp.sqrt(square))
    coulomb = jnp.concatenate(factors, axis=1)

    wait_bytes(grecv.at[:15], gsem.at[1])
    pencil = jnp.concatenate(
        [grecv[:, 16 * unit : 16 * unit + 16, :].reshape(256, 128) for unit in range(3)], axis=1
    )
    spectral = dot3_table_left(pair_of("forward_x"), pencil) * coulomb
    restored = dot3_table_left(pair_of("plain"), spectral)
    for unit in range(3):
        wsend[unit] = restored[:, 128 * unit : 128 * unit + 128]

    for k in (4, 3, 5, 2, 6, 1, 7):
        to_space = lax.rem(space + k, 8)
        row = pl.multiple_of(24 * to_space, 8)
        send(
            wsend.at[:, pl.ds(row, 24)], wrecv.at[pl.ds(3 * space, 3)],
            wsem.at[0], wsem.at[1], band, to_space,
        )
    wrecv[pl.ds(3 * space, 3)] = wsend[:, pl.ds(pl.multiple_of(24 * space, 8), 24), :]
    brow[...] = jnp.zeros(brow.shape, F32)
    wait_bytes(wrecv.at[:21], wsem.at[1])

    for unit in range(24):
        brow[unit % 2, pl.ds(unit // 2, 24, stride=16), :] = wrecv[unit]
    rows = jnp.concatenate([brow[0], brow[1]], axis=1)
    zsend[...] = dot3_table_left(pair_of("inverse_y"), rows, ((1,), (1,)))

    for k in (4, 12, 8, 3, 5, 11, 13, 2, 6, 10, 14, 7, 9, 1, 15):
        to = lax.rem(band + k, 16)
        send(
            zsend.at[pl.ds(pl.multiple_of(16 * to, 8), 16)], zrecv.at[band],
            zsem.at[0], zsem.at[1], to, space,
        )
    zrecv[band] = zsend[pl.ds(pl.multiple_of(16 * band, 8), 16), :]
    wait_bytes(zrecv.at[:15], zsem.at[1])

    granule = lax.broadcasted_iota(jnp.int32, (16, 128), 1) // 16
    for third in range(3):
        for side in range(2):
            blocks = [zrecv[8 * side + i, :, 128 * third : 128 * third + 128] for i in range(8)]
            for bit in (1, 2, 4):
                upper = lax.rem(granule // bit, 2) == 1
                after = list(blocks)
                for i in range(8):
                    if not i & bit:
                        low, high = blocks[i], blocks[i | bit]
                        after[i] = jnp.where(upper, pltpu.roll(high, 16 * bit, 1), low)
                        after[i | bit] = jnp.where(upper, high, pltpu.roll(low, 128 - 16 * bit, 1))
                blocks = after
            for i in range(8):
                x = 8 * third + i
                mat[16 * x : 16 * x + 16, 128 * side : 128 * side + 128] = blocks[i]
    result = dot3_table_right(mat[...], pair_of("inverse_z"))
    for x in range(SLAB):
        out[0, x] = result[16 * x : 16 * x + 12]

    wait_bytes(psend.at[:, :PIECE], sent.at[0])
    wait_bytes(osend, sent.at[1])
    wait_bytes(other, sent.at[2])
    wait_bytes(ya_recv, sent.at[3])
    wait_bytes(xb_recv, sent.at[4])
    wait_bytes(xa_recv, sent.at[5])
    wait_bytes(yb_recv, sent.at[6])
    wait_bytes(precv.at[0, : 6 * PIECE], sent.at[7])
    wait_bytes(precv.at[0, : 8 * PIECE], sent.at[8])
    wait_bytes(grecv.at[:15], gsem.at[0])
    wait_bytes(wrecv.at[:21], wsem.at[0])
    wait_bytes(zrecv.at[:15], zsem.at[0])


def on_device(orbitals, occupations, shifts, perturbations, local_potential):
    any_space = pl.BlockSpec(memory_space=pl.ANY)
    smem = pl.BlockSpec(memory_space=pltpu.SMEM)
    vmem = pl.BlockSpec(memory_space=pltpu.VMEM)
    dma = pltpu.SemaphoreType.DMA
    return pl.pallas_call(
        kernel,
        out_shape=jax.ShapeDtypeStruct((1, SLAB, 12, NG), F32),
        in_specs=[smem] * 2 + [any_space] * 4,
        out_specs=vmem,
        scratch_shapes=[
            pltpu.VMEM(TABLE.shape, BF16),
            pltpu.VMEM((EXT, NG, NG), BF16),
            pltpu.VMEM((EXT, NG, NG), F32),
            pltpu.VMEM((SLAB, NG, NG), F32),
            pltpu.VMEM((EXT, NG, NG), F32),
            pltpu.VMEM((EXT + 8, NG, NG), F32),
            pltpu.VMEM((2, 4, ROWS, 128), F32),
            pltpu.VMEM((2, 4, ROWS, 128), F32),
            pltpu.VMEM((2, ROWS, 128), F32),
            pltpu.VMEM((2, 4 * ROWS, 128), F32),
            pltpu.VMEM((8, 2, NG, NG), F32),
            pltpu.VMEM((8, 2, NG, NG), F32),
            pltpu.VMEM((8, 2, NG, NG), F32),
            pltpu.VMEM((8, 3, 4, 2, 24, 128), F32),
            pltpu.VMEM((4, 3, 3, 2, 24, 128), F32),
            pltpu.VMEM((4, 3, 2, 24, 128), F32),
            pltpu.VMEM((4, 3, 24, 128), F32),
            pltpu.VMEM((4, 3, 4, 24, 128), F32),
            pltpu.VMEM((4, 3, 4, 24, 128), F32),
            pltpu.VMEM((4, 3, 3, 24, 128), F32),
            pltpu.VMEM((8, 3, 24, 128), F32),
            pltpu.VMEM((768, 128), F32),
            pltpu.VMEM((16, 48, 128), F32),
            pltpu.VMEM((3, NG, 128), F32),
            pltpu.VMEM((24, 24, 128), F32),
            pltpu.VMEM((2, 384, 128), F32),
            pltpu.VMEM((256, 384), F32),
            pltpu.VMEM((16, 16, 384), F32),
            pltpu.VMEM((384, 256), F32),
            dma((8,)),
            dma((2, 2)),
            dma((2,)),
            dma((2,)),
            dma((8,)),
            dma((4,)),
            dma((4,)),
            dma((4,)),
            dma((4,)),
            dma((2,)),
            dma((2,)),
            dma((2,)),
            dma((9,)),
        ],
        compiler_params=pltpu.CompilerParams(
            collective_id=0, has_side_effects=True, vmem_limit_bytes=60 * 2**20
        ),
        name="response",
    )(occupations, shifts, orbitals, perturbations, local_potential, jnp.asarray(TABLE))


def solution(mesh):
    in_specs = (
        P("band", "space", None, None),
        P("band"),
        P("band"),
        P(None, "space", None, None),
        P("space", None, None),
    )
    out_specs = P(None, "space", "band", None)
    return jax.shard_map(
        on_device, mesh=mesh, in_specs=in_specs, out_specs=out_specs, check_vma=False
    )
```

```python
import math

import jax
import jax.numpy as jnp
import numpy as np
from jax import lax
from jax.experimental import pallas as pl
from jax.experimental.pallas import tpu as pltpu
from jax.sharding import PartitionSpec as P

MESH = pl.DeviceIdType.MESH
BF16 = jnp.bfloat16
F32 = jnp.float32
NG = 192
SLAB = 24
EXT = 32
COEFFS = (-205.0 / 72.0, 8.0 / 5.0, -1.0 / 5.0, 8.0 / 315.0, -1.0 / 560.0)
WEIGHTS = (8064.0, -1008.0, 128.0, -9.0)
ROWS = 288
PIECE = 4 * ROWS // 8
CHUNKS = (
    (0, 80, ((0, 184, 8), (8, 0, 72))),
    (120, 64, ((0, 72, 64),)),
    (216, 48, ((0, 136, 48),)),
)
ITEMS = ((0, 0), (1, 0), (2, 0), (0, 1), (0, 2), (0, 3), (1, 1), (1, 2), (1, 3), (2, 3), (2, 1), (2, 2))
X_FIRST = (9, 11)
Y_FIRST = tuple(n for n in range(12) if n not in X_FIRST)


def cas(product):
    angles = (np.asarray(product, np.int64) % NG).astype(np.float64) * (2.0 * math.pi / NG)
    return np.cos(angles) + np.sin(angles)


def halves(table):
    table = np.asarray(table, np.float32)
    high = table.astype(jnp.bfloat16)
    low = (table - high.astype(np.float32)).astype(jnp.bfloat16)
    return np.stack([high, low])


def tables():
    index = np.arange(NG)
    plain = cas(index[:, None] * index[None, :])
    stencil = np.zeros((NG, NG), np.float32)
    for offset, weight in enumerate(WEIGHTS, 1):
        for sign in (1, -1):
            stencil[index, (index + sign * offset) % NG] += weight
    window = np.zeros((64, 80), np.float32)
    for offset, weight in enumerate(WEIGHTS, 1):
        for sign in (1, -1):
            window[np.arange(64), np.arange(64) + 8 + sign * offset] += weight
    forward_y = np.zeros((2, 384, 256))
    for layer in range(2):
        for chunk in range(3):
            first = 128 * chunk + 64 * layer
            forward_y[layer, first : first + 64, :NG] = plain[64 * chunk : 64 * chunk + 64]
    forward_x = np.zeros((NG, 256))
    for core in range(2):
        for space in range(8):
            for slot in range(16):
                block, layer = divmod(slot, 4)
                ext = (12 - 4 * block if core == 0 else 16 + 4 * block) + layer
                x = (SLAB * space + ext - 4) % NG
                column = 128 * (slot // 8) + (core * 8 + space) * 8 + slot % 8
                forward_x[:, column] = plain[:, x]
    inverse_y = np.zeros((256, 256))
    inverse_z = np.zeros((256, NG))
    for band in range(16):
        inverse_y[band * 16 : band * 16 + 12, :NG] = plain[band * 12 : band * 12 + 12]
        x_lo, y, core = band // 8, (band // 2) % 4, band % 2
        first = 24 * (2 * y + x_lo) + 12 * core
        inverse_z[band * 16 : band * 16 + 12] = plain[first : first + 12]
    pieces = {
        "stencil": stencil.astype(jnp.bfloat16)[None],
        "window": window.astype(jnp.bfloat16)[None],
        "plain": halves(plain),
        "forward_y0": halves(forward_y[0]),
        "forward_y1": halves(forward_y[1]),
        "forward_x": halves(forward_x),
        "inverse_y": halves(inverse_y),
        "inverse_z": halves(inverse_z),
    }
    where, rows, start = {}, [], 0
    for name, piece in pieces.items():
        count, height, width = piece.shape
        where[name] = (start, count, height, width)
        flat = piece.reshape(count * height, width)
        rows.append(np.pad(flat, ((0, 0), (0, 256 - width))))
        start += count * height
    return where, np.concatenate(rows)


WHERE, TABLE = tables()


def split(value):
    high = value.astype(BF16)
    low = (value - high.astype(F32)).astype(BF16)
    return high, low


def dot(a, b, dims=((1,), (0,))):
    return lax.dot_general(a, b, (dims, ((), ())), preferred_element_type=F32)


def dot3_table_left(table, value, dims=((1,), (0,))):
    high, low = split(value)
    return dot(table[0], high, dims) + (dot(table[1], high, dims) + dot(table[0], low, dims))


def dot3_table_right(value, table):
    high, low = split(value)
    return dot(high, table[0]) + (dot(low, table[0]) + dot(high, table[1]))


def pack_into(ref, index, layer):
    for start, count, places in CHUNKS:
        rows = [layer[row : row + size] for _, row, size in places]
        rows = rows[0] if len(rows) == 1 else jnp.concatenate(rows, axis=0)
        half = count // 2
        ref[index, start : start + count, :] = rows[:, :128]
        ref[index, start + count : start + count + half, :64] = rows[:half, 128:]
        ref[index, start + count : start + count + half, 64:] = rows[half:, 128:]


def unpack_into(ref, where, chunk, main, tail):
    _, count, places = CHUNKS[chunk]
    half = count // 2
    for at, row, size in places:
        ref[*where, row : row + size, :128] = main[at : at + size]
        for lo, hi, lane in ((0, half, 0), (half, count, 64)):
            first, last = max(at, lo), min(at + size, hi)
            if first < last:
                ref[*where, row + first - at : row + last - at, 128:] = tail[
                    first - lo : last - lo, lane : lane + 64
                ]


def kernel(
    occ_ref, shift_ref, orb_hbm, pert_hbm, pot_hbm, table_hbm, out,
    table, orb, pert, pot, v, e,
    osend, orecv, psend, precv, orb_halo, v_halo,
    mine, other, crecv, tiles, ya_recv, xsum, xb_recv, xa_recv, ysum, yb_recv, red,
    gsend, grecv, wsend, wrecv, brow, zsend, zrecv, mat,
    load_sem, osem, psem, fsem, csem, ya_sem, xb_sem, xa_sem, yb_sem, gsem, wsem, zsem, sent,
):
    band = lax.axis_index("band")
    space = lax.axis_index("space")
    core = lax.rem(band, 2)
    y = lax.rem(band // 2, 4)
    x_lo = band // 8
    group = 2 * y + x_lo
    up = lax.rem(space + 1, 8)
    down = lax.rem(space + 7, 8)

    def band_of(x, yy, c):
        return x * 8 + yy * 2 + c

    def y_at(k):
        return lax.rem(y + k, 4)

    def part(name, number=0):
        start, _, height, width = WHERE[name]
        return table[start + number * height : start + (number + 1) * height, :width]

    def pair_of(name):
        return part(name, 0), part(name, 1)

    def wait_bytes(ref, sem):
        pltpu.make_async_copy(ref, ref, sem).wait()

    def send(src, dst, send_sem, recv_sem, to_band, to_space):
        pltpu.make_async_remote_copy(
            src_ref=src,
            dst_ref=dst,
            send_sem=send_sem,
            recv_sem=recv_sem,
            device_id=(to_band, to_space),
            device_id_type=MESH,
        ).start()

    loads = []
    for number, (source, target) in enumerate(
        (
            (pert_hbm.at[0, 0:4], pert.at[4:8]),
            (pert_hbm.at[0, 20:24], pert.at[24:28]),
            (orb_hbm.at[0, 0:4], orb.at[4:8]),
            (orb_hbm.at[0, 20:24], orb.at[24:28]),
            (orb_hbm.at[0, 4:20], orb.at[8:24]),
            (pert_hbm.at[0, 4:20], pert.at[8:24]),
            (pot_hbm, pot),
            (table_hbm, table),
        )
    ):
        copy = pltpu.make_async_copy(source, target, load_sem.at[number])
        copy.start()
        loads.append(copy)

    barrier = pltpu.get_barrier_semaphore()
    for k in range(1, 8):
        for c in range(2):
            pl.semaphore_signal(
                barrier,
                inc=1,
                device_id=(band_of(x_lo, y, c), lax.rem(space + k, 8)),
                device_id_type=MESH,
            )
    for k in range(1, 16):
        pl.semaphore_signal(
            barrier, inc=1, device_id=(lax.rem(band + k, 16), space), device_id_type=MESH
        )

    for layer in list(range(0, 8)) + list(range(32, 40)):
        e[layer] = jnp.zeros((NG, NG), F32)
    for layer in (0, 1, 2, 3, 28, 29, 30, 31):
        v[layer] = jnp.zeros((NG, NG), F32)

    delta = 5.5
    shift = jnp.full((1, NG), shift_ref[0], F32)
    theta = shift + 5.5
    ratio = theta / delta
    w0 = 1.0 / ratio
    w1 = 1.0 / (2.0 * ratio - w0)
    w2 = 1.0 / (2.0 * ratio - w1)
    beta1, beta = 2.0 * w1 / delta, 2.0 * w2 / delta
    a_own = w1 * w0 / theta + beta1
    b_own = beta1 / theta
    b_sten = b_own / 10080.0
    q_shift = shift - 1.5 * COEFFS[0]
    g0 = (1.0 - w2 * w0) / theta
    g1 = 1.0 + w2 * w1 + beta / beta1
    beta_sten = beta / 10080.0
    factor = jnp.full((1, NG), occ_ref[0], F32) * (-4.0 / 16.0)

    piece = 4 * core + y
    piece_row = pl.multiple_of(piece * PIECE, 8)
    half_row = pl.multiple_of(lax.rem(piece, 2) * PIECE, 8)
    loads[0].wait()
    loads[1].wait()
    pack_into(psend, 0, pert[24 + piece // 2])
    pack_into(psend, 1, pert[4 + piece // 2])
    loads[2].wait()
    loads[3].wait()

    pl.semaphore_wait(barrier, 29)

    for way, target in ((0, up), (1, down)):
        send(
            psend.at[way, pl.ds(half_row, PIECE)],
            precv.at[way, pl.ds(piece_row, PIECE)],
            sent.at[0], psem.at[way], band, target,
        )
    for way in range(2):
        for layer in range(4):
            pack_into(osend.at[way], layer, orb[(24 if way == 0 else 4) + layer].astype(F32))
    for chunk, (start, count, _) in enumerate(CHUNKS):
        for way, target in ((0, up), (1, down)):
            send(
                osend.at[way, :, start : start + 3 * count // 2],
                orecv.at[way, :, start : start + 3 * count // 2],
                sent.at[1], osem.at[way, chunk], band, target,
            )

    loads[4].wait()
    loads[5].wait()

    def make_v(layer, carry):
        v[layer] = orb[layer].astype(F32) * pert[layer]
        return carry

    lax.fori_loop(4, 28, make_v, 0)
    loads[6].wait()
    loads[7].wait()

    def along_x(ref, layer, rows):
        total = WEIGHTS[0] * (ref[layer - 1, rows] + ref[layer + 1, rows])
        for offset in range(2, 5):
            total += WEIGHTS[offset - 1] * (
                ref[layer - offset, rows] + ref[layer + offset, rows]
            )
        return total

    def make_e(layer, carry):
        value = v[layer + 4]
        high, low = split(value)
        stencil = part("stencil")
        total = along_x(v, layer + 4, slice(None))
        total += dot(high, stencil) + dot(low, stencil)
        total += dot(stencil, high) + dot(stencil, low)
        diagonal = pot[layer] + q_shift
        e[layer + 8] = (a_own - b_own * diagonal) * value + b_sten * total
        return carry

    def density_own(layer, chunk):
        rows = slice(64 * chunk, 64 * chunk + 64)
        around = {0: ((184, 192), (0, 72)), 1: ((56, 136),), 2: ((120, 192), (0, 8))}[chunk]
        pieces = [e[layer + 4, lo:hi] for lo, hi in around]
        high, low = split(pieces[0] if len(pieces) == 1 else jnp.concatenate(pieces, axis=0))
        window = part("window")
        total = along_x(e, layer + 4, rows) + (dot(window, high) + dot(window, low))
        value = e[layer + 4, rows]
        high, low = split(value)
        stencil = part("stencil")
        total += dot(high, stencil) + dot(low, stencil)
        diagonal = pot[layer - 4, rows] + q_shift
        solved = g0 * v[layer, rows] + (g1 - beta * diagonal) * value + beta_sten * total
        return factor * orb[layer, rows].astype(F32) * solved

    def density_beyond(layer, chunk):
        rows = slice(64 * chunk, 64 * chunk + 64)
        at = jnp.where(layer < 4, layer, layer - 24)
        return factor * orb_halo[at, rows] * (beta_sten * along_x(e, layer + 4, rows))

    def make_item(n):
        chunk, block = ITEMS[n]
        density = density_beyond if block == 3 else density_own

        def fill(ref, c):
            base = jnp.where(c == 0, 12 - 4 * block, 16 + 4 * block)

            def body(layer, carry):
                ref[n, layer] = density(base + layer, chunk)
                return carry

            lax.fori_loop(0, 4, body, 0)

        fill(other, 1 - core)
        send(
            other.at[n], crecv.at[n], sent.at[2], csem.at[n], band_of(x_lo, y, 1 - core), space
        )
        fill(mine, core)

    def add_cores(n):
        wait_bytes(crecv.at[n], csem.at[n])
        high, low = split((mine[n] + crecv[n]).reshape(256, NG))
        table_high, table_low = pair_of("plain")
        last = ((1,), (1,))
        rows = dot(table_high, high, last) + (
            dot(table_low, high, last) + dot(table_high, low, last)
        )
        for slot in range(2):
            tiles[n, slot] = rows[:, 128 * slot : 128 * slot + 128].reshape(4, 2, 24, 128)

    def ya_start(n):
        add_cores(n)
        i = Y_FIRST.index(n)
        for k in (2, 1, 3):
            send(
                tiles.at[n, :, y_at(k)], ya_recv.at[i, k - 1],
                sent.at[3], ya_sem.at[i], band_of(x_lo, y_at(k), core), space,
            )

    def ya_end(n):
        i = Y_FIRST.index(n)
        wait_bytes(ya_recv.at[i], ya_sem.at[i])
        xsum[i] = (tiles[n, :, y] + ya_recv[i, 0]) + (ya_recv[i, 1] + ya_recv[i, 2])
        send(
            xsum.at[i, :, 1 - x_lo], xb_recv.at[i],
            sent.at[4], xb_sem.at[i], band_of(1 - x_lo, y, core), space,
        )

    def xb_end(n):
        i = Y_FIRST.index(n)
        chunk, block = ITEMS[n]
        wait_bytes(xb_recv.at[i], xb_sem.at[i])
        red[chunk, block] = xsum[i, :, x_lo] + xb_recv[i]

    def xa_start(n):
        add_cores(n)
        i = X_FIRST.index(n)
        send(
            tiles.at[n, :, :, 1 - x_lo], xa_recv.at[i],
            sent.at[5], xa_sem.at[i], band_of(1 - x_lo, y, core), space,
        )

    def xa_end(n):
        i = X_FIRST.index(n)
        wait_bytes(xa_recv.at[i], xa_sem.at[i])
        ysum[i] = tiles[n, :, :, x_lo] + xa_recv[i]
        for k in (2, 1, 3):
            send(
                ysum.at[i, :, y_at(k)], yb_recv.at[i, k - 1],
                sent.at[6], yb_sem.at[i], band_of(x_lo, y_at(k), core), space,
            )

    def yb_end(n):
        i = X_FIRST.index(n)
        chunk, block = ITEMS[n]
        wait_bytes(yb_recv.at[i], yb_sem.at[i])
        red[chunk, block] = (ysum[i, :, y] + yb_recv[i, 0]) + (yb_recv[i, 1] + yb_recv[i, 2])

    lax.fori_loop(4, 12, make_e, 0)

    for way in range(2):
        wait_bytes(precv.at[way, :PIECE], psem.at[way])
    for way in range(2):
        for k in (2, 1, 3):
            send(
                precv.at[way, pl.ds(piece_row, PIECE)],
                precv.at[way, pl.ds(piece_row, PIECE)],
                sent.at[7], fsem.at[0], band_of(x_lo, y_at(k), core), space,
            )
    lax.fori_loop(12, 20, make_e, 0)
    make_item(0)
    wait_bytes(precv.at[0, : 6 * PIECE], fsem.at[0])
    core_row = pl.multiple_of(core * 4 * PIECE, 8)
    for way in range(2):
        send(
            precv.at[way, pl.ds(core_row, 4 * PIECE)],
            precv.at[way, pl.ds(core_row, 4 * PIECE)],
            sent.at[8], fsem.at[1], band_of(x_lo, y, 1 - core), space,
        )
    make_item(1)
    ya_start(0)
    make_item(2)
    ya_start(1)
    lax.fori_loop(0, 4, make_e, 0)
    ya_start(2)
    lax.fori_loop(20, 24, make_e, 0)

    def take_halo(chunk):
        start, count, places = CHUNKS[chunk]
        half = count // 2
        for way in range(2):
            wait_bytes(orecv.at[way, :, start : start + count + half], osem.at[way, chunk])
            for layer in range(4):
                main = orecv[way, layer, start : start + count]
                tail = orecv[way, layer, start + count : start + count + half]
                row = layer * ROWS + start
                unpack_into(orb_halo, (4 * way + layer,), chunk, main, tail)
                main = main * precv[way, row : row + count]
                tail = tail * precv[way, row + count : row + count + half]
                unpack_into(v_halo, (4 * way + layer,), chunk, main, tail)
        for _, row, size in places:
            rows = slice(row, row + size)
            for x in range(4):
                below = WEIGHTS[3] * v_halo[x, rows]
                for layer in range(x + 1, 4):
                    below += WEIGHTS[3 + x - layer] * v_halo[layer, rows]
                e[x + 8, rows] += b_sten * below
                above = WEIGHTS[3] * v_halo[4 + x, rows]
                for layer in range(x):
                    above += WEIGHTS[3 + layer - x] * v_halo[4 + layer, rows]
                e[x + 28, rows] += b_sten * above

    wait_bytes(precv.at[0, : 8 * PIECE], fsem.at[1])
    take_halo(0)
    make_item(3)
    make_item(4)
    ya_start(3)
    make_item(5)
    ya_start(4)
    ya_start(5)
    for n in range(0, 3):
        ya_end(n)
    take_halo(1)
    make_item(6)
    make_item(7)
    ya_start(6)
    make_item(8)
    ya_start(7)
    ya_start(8)
    for n in range(3, 6):
        ya_end(n)
    take_halo(2)
    make_item(9)
    make_item(10)
    xa_start(9)
    make_item(11)
    ya_start(10)
    xa_start(11)
    for n in range(6, 9):
        ya_end(n)
    xa_end(9)
    for n in range(0, 6):
        xb_end(n)

    mine_at = core * 8 + space

    def to_columns(side):
        blocks = slice(2 * side, 2 * side + 2)
        value = jnp.concatenate(
            [red[chunk, blocks].reshape(96, 128) for chunk in range(3)], axis=1
        )
        high, low = split(value)
        for layer in range(2):
            table_high, table_low = pair_of("forward_y%d" % layer)
            columns = dot(high, table_high) + (dot(low, table_high) + dot(high, table_low))
            for j in range(4):
                for half in range(2):
                    gsend[side, pl.ds(half * 8 + 2 * j + layer, 24, stride=16), :] = columns[
                        24 * j : 24 * j + 24, 128 * half : 128 * half + 128
                    ]
        for k in (4, 3, 5, 2, 6, 1, 7, 0):
            for c in range(2):
                if (k, c) != (0, 0):
                    to_space = lax.rem(space + k, 8)
                    to_core = lax.rem(core + c, 2)
                    row = pl.multiple_of(24 * (to_core * 8 + to_space), 8)
                    send(
                        gsend.at[side, pl.ds(row, 24)], grecv.at[side, mine_at],
                        gsem.at[2], gsem.at[side], band_of(x_lo, y, to_core), to_space,
                    )
        grecv[side, mine_at] = gsend[side, pl.ds(pl.multiple_of(24 * mine_at, 8), 24), :]

    ya_end(10)
    xa_end(11)
    for n in (6, 7, 8, 10):
        xb_end(n)
    to_columns(0)
    yb_end(9)
    yb_end(11)
    to_columns(1)

    kx = lax.broadcasted_iota(jnp.int32, (NG, 128), 0)
    lane = lax.broadcasted_iota(jnp.int32, (NG, 128), 1)
    gx = jnp.minimum(kx, NG - kx)
    factors = []
    for unit in range(3):
        number = 3 * mine_at + unit
        kz = 24 * group + number // 2
        gz = jnp.minimum(kz, NG - kz)
        ky = lane + 128 * lax.rem(number, 2)
        gy = jnp.minimum(ky, NG - ky)
        square = (gx * gx + gy * gy + (gz * gz + 1)).astype(F32)
        factors.append((256.0 / float(NG) ** 3) / jnp.sqrt(square))
    coulomb = jnp.concatenate(factors, axis=1)

    for side in range(2):
        wait_bytes(grecv.at[side, :15], gsem.at[side])
    pencil = jnp.concatenate(
        [grecv[:, :, 8 * unit : 8 * unit + 8, :].reshape(256, 128) for unit in range(3)], axis=1
    )
    spectral = dot3_table_left(pair_of("forward_x"), pencil) * coulomb
    restored = dot3_table_left(pair_of("plain"), spectral)
    for unit in range(3):
        wsend[unit] = restored[:, 128 * unit : 128 * unit + 128]

    for k in (4, 3, 5, 2, 6, 1, 7):
        to_space = lax.rem(space + k, 8)
        row = pl.multiple_of(24 * to_space, 8)
        send(
            wsend.at[:, pl.ds(row, 24)], wrecv.at[pl.ds(3 * space, 3)],
            wsem.at[0], wsem.at[1], band, to_space,
        )
    wrecv[pl.ds(3 * space, 3)] = wsend[:, pl.ds(pl.multiple_of(24 * space, 8), 24), :]
    brow[...] = jnp.zeros(brow.shape, F32)
    wait_bytes(wrecv.at[:21], wsem.at[1])

    for unit in range(24):
        brow[unit % 2, pl.ds(unit // 2, 24, stride=16), :] = wrecv[unit]
    rows = jnp.concatenate([brow[0], brow[1]], axis=1)
    zsend[...] = dot3_table_left(pair_of("inverse_y"), rows, ((1,), (1,)))

    for k in (4, 12, 8, 3, 5, 11, 13, 2, 6, 10, 14, 7, 9, 1, 15):
        to = lax.rem(band + k, 16)
        send(
            zsend.at[pl.ds(pl.multiple_of(16 * to, 8), 16)], zrecv.at[band],
            zsem.at[0], zsem.at[1], to, space,
        )
    zrecv[band] = zsend[pl.ds(pl.multiple_of(16 * band, 8), 16), :]
    wait_bytes(zrecv.at[:15], zsem.at[1])

    granule = lax.broadcasted_iota(jnp.int32, (16, 128), 1) // 16
    for third in range(3):
        for side in range(2):
            blocks = [zrecv[8 * side + i, :, 128 * third : 128 * third + 128] for i in range(8)]
            for bit in (1, 2, 4):
                upper = lax.rem(granule // bit, 2) == 1
                after = list(blocks)
                for i in range(8):
                    if not i & bit:
                        low, high = blocks[i], blocks[i | bit]
                        after[i] = jnp.where(upper, pltpu.roll(high, 16 * bit, 1), low)
                        after[i | bit] = jnp.where(upper, high, pltpu.roll(low, 128 - 16 * bit, 1))
                blocks = after
            for i in range(8):
                x = 8 * third + i
                mat[16 * x : 16 * x + 16, 128 * side : 128 * side + 128] = blocks[i]
    result = dot3_table_right(mat[...], pair_of("inverse_z"))
    for x in range(SLAB):
        out[0, x] = result[16 * x : 16 * x + 12]

    wait_bytes(psend.at[:, :PIECE], sent.at[0])
    wait_bytes(osend, sent.at[1])
    wait_bytes(other, sent.at[2])
    wait_bytes(ya_recv, sent.at[3])
    wait_bytes(xb_recv, sent.at[4])
    wait_bytes(xa_recv, sent.at[5])
    wait_bytes(yb_recv, sent.at[6])
    wait_bytes(precv.at[0, : 6 * PIECE], sent.at[7])
    wait_bytes(precv.at[0, : 8 * PIECE], sent.at[8])
    wait_bytes(grecv.at[:, :15], gsem.at[2])
    wait_bytes(wrecv.at[:21], wsem.at[0])
    wait_bytes(zrecv.at[:15], zsem.at[0])


def on_device(orbitals, occupations, shifts, perturbations, local_potential):
    any_space = pl.BlockSpec(memory_space=pl.ANY)
    smem = pl.BlockSpec(memory_space=pltpu.SMEM)
    vmem = pl.BlockSpec(memory_space=pltpu.VMEM)
    dma = pltpu.SemaphoreType.DMA
    return pl.pallas_call(
        kernel,
        out_shape=jax.ShapeDtypeStruct((1, SLAB, 12, NG), F32),
        in_specs=[smem] * 2 + [any_space] * 4,
        out_specs=vmem,
        scratch_shapes=[
            pltpu.VMEM(TABLE.shape, BF16),
            pltpu.VMEM((EXT, NG, NG), BF16),
            pltpu.VMEM((EXT, NG, NG), F32),
            pltpu.VMEM((SLAB, NG, NG), F32),
            pltpu.VMEM((EXT, NG, NG), F32),
            pltpu.VMEM((EXT + 8, NG, NG), F32),
            pltpu.VMEM((2, 4, ROWS, 128), F32),
            pltpu.VMEM((2, 4, ROWS, 128), F32),
            pltpu.VMEM((2, ROWS, 128), F32),
            pltpu.VMEM((2, 4 * ROWS, 128), F32),
            pltpu.VMEM((8, NG, NG), F32),
            pltpu.VMEM((8, NG, NG), F32),
            pltpu.VMEM((12, 4, 64, NG), F32),
            pltpu.VMEM((12, 4, 64, NG), F32),
            pltpu.VMEM((12, 4, 64, NG), F32),
            pltpu.VMEM((12, 2, 4, 2, 24, 128), F32),
            pltpu.VMEM((10, 3, 2, 2, 24, 128), F32),
            pltpu.VMEM((10, 2, 2, 24, 128), F32),
            pltpu.VMEM((10, 2, 24, 128), F32),
            pltpu.VMEM((2, 2, 4, 24, 128), F32),
            pltpu.VMEM((2, 2, 4, 24, 128), F32),
            pltpu.VMEM((2, 3, 2, 24, 128), F32),
            pltpu.VMEM((3, 4, 2, 24, 128), F32),
            pltpu.VMEM((2, 384, 128), F32),
            pltpu.VMEM((2, 16, 24, 128), F32),
            pltpu.VMEM((3, NG, 128), F32),
            pltpu.VMEM((24, 24, 128), F32),
            pltpu.VMEM((2, 384, 128), F32),
            pltpu.VMEM((256, 384), F32),
            pltpu.VMEM((16, 16, 384), F32),
            pltpu.VMEM((384, 256), F32),
            dma((8,)),
            dma((2, 3)),
            dma((2,)),
            dma((2,)),
            dma((12,)),
            dma((10,)),
            dma((10,)),
            dma((2,)),
            dma((2,)),
            dma((3,)),
            dma((2,)),
            dma((2,)),
            dma((9,)),
        ],
        compiler_params=pltpu.CompilerParams(
            collective_id=0, has_side_effects=True, vmem_limit_bytes=60 * 2**20
        ),
        name="response",
    )(occupations, shifts, orbitals, perturbations, local_potential, jnp.asarray(TABLE))


def solution(mesh):
    in_specs = (
        P("band", "space", None, None),
        P("band"),
        P("band"),
        P(None, "space", None, None),
        P("space", None, None),
    )
    out_specs = P(None, "space", "band", None)
    return jax.shard_map(
        on_device, mesh=mesh, in_specs=in_specs, out_specs=out_specs, check_vma=False
    )
```

```python
import math

import jax
import jax.numpy as jnp
import numpy as np
from jax import lax
from jax.experimental import pallas as pl
from jax.experimental.pallas import tpu as pltpu
from jax.sharding import PartitionSpec as P

MESH = pl.DeviceIdType.MESH
BF16 = jnp.bfloat16
F32 = jnp.float32
NG = 192
SLAB = 24
EXT = 32
COEFFS = (-205.0 / 72.0, 8.0 / 5.0, -1.0 / 5.0, 8.0 / 315.0, -1.0 / 560.0)
WEIGHTS = (8064.0, -1008.0, 128.0, -9.0)
ROWS = 288
PIECE = 4 * ROWS // 8
CHUNKS = (
    (0, 80, ((0, 184, 8), (8, 0, 72))),
    (120, 64, ((0, 72, 64),)),
    (216, 48, ((0, 136, 48),)),
)
ITEMS = ((0, 0), (1, 0), (2, 0), (0, 1), (0, 2), (0, 3), (1, 1), (1, 2), (1, 3), (2, 3), (2, 1), (2, 2))
X_FIRST = (9, 11)
Y_FIRST = tuple(n for n in range(12) if n not in X_FIRST)


def cas(product):
    angles = (np.asarray(product, np.int64) % NG).astype(np.float64) * (2.0 * math.pi / NG)
    return np.cos(angles) + np.sin(angles)


def halves(table):
    table = np.asarray(table, np.float32)
    high = table.astype(jnp.bfloat16)
    low = (table - high.astype(np.float32)).astype(jnp.bfloat16)
    return np.stack([high, low])


def tables():
    index = np.arange(NG)
    plain = cas(index[:, None] * index[None, :])
    stencil = np.zeros((NG, NG), np.float32)
    for offset, weight in enumerate(WEIGHTS, 1):
        for sign in (1, -1):
            stencil[index, (index + sign * offset) % NG] += weight
    window = np.zeros((64, 80), np.float32)
    for offset, weight in enumerate(WEIGHTS, 1):
        for sign in (1, -1):
            window[np.arange(64), np.arange(64) + 8 + sign * offset] += weight
    forward_y = np.zeros((2, 384, 256))
    for layer in range(2):
        for chunk in range(3):
            first = 128 * chunk + 64 * layer
            forward_y[layer, first : first + 64, :NG] = plain[64 * chunk : 64 * chunk + 64]
    forward_x = np.zeros((NG, 256))
    for core in range(2):
        for space in range(8):
            for slot in range(16):
                block, layer = divmod(slot, 4)
                ext = (12 - 4 * block if core == 0 else 16 + 4 * block) + layer
                x = (SLAB * space + ext - 4) % NG
                column = 128 * (slot // 8) + (core * 8 + space) * 8 + slot % 8
                forward_x[:, column] = plain[:, x]
    inverse_y = np.zeros((256, 256))
    inverse_z = np.zeros((256, NG))
    for band in range(16):
        inverse_y[band * 16 : band * 16 + 12, :NG] = plain[band * 12 : band * 12 + 12]
        x_lo, y, core = band // 8, (band // 2) % 4, band % 2
        first = 24 * (2 * y + x_lo) + 12 * core
        inverse_z[band * 16 : band * 16 + 12] = plain[first : first + 12]
    pieces = {
        "stencil": stencil.astype(jnp.bfloat16)[None],
        "window": window.astype(jnp.bfloat16)[None],
        "plain": halves(plain),
        "forward_y0": halves(forward_y[0]),
        "forward_y1": halves(forward_y[1]),
        "forward_x": halves(forward_x),
        "inverse_y": halves(inverse_y),
        "inverse_z": halves(inverse_z),
    }
    where, rows, start = {}, [], 0
    for name, piece in pieces.items():
        count, height, width = piece.shape
        where[name] = (start, count, height, width)
        flat = piece.reshape(count * height, width)
        rows.append(np.pad(flat, ((0, 0), (0, 256 - width))))
        start += count * height
    return where, np.concatenate(rows)


WHERE, TABLE = tables()


def split(value):
    high = value.astype(BF16)
    low = (value - high.astype(F32)).astype(BF16)
    return high, low


def dot(a, b, dims=((1,), (0,))):
    return lax.dot_general(a, b, (dims, ((), ())), preferred_element_type=F32)


def dot3_table_left(table, value, dims=((1,), (0,))):
    high, low = split(value)
    return dot(table[0], high, dims) + (dot(table[1], high, dims) + dot(table[0], low, dims))


def dot3_table_right(value, table):
    high, low = split(value)
    return dot(high, table[0]) + (dot(low, table[0]) + dot(high, table[1]))


def pack_into(ref, index, layer):
    for start, count, places in CHUNKS:
        rows = [layer[row : row + size] for _, row, size in places]
        rows = rows[0] if len(rows) == 1 else jnp.concatenate(rows, axis=0)
        half = count // 2
        ref[index, start : start + count, :] = rows[:, :128]
        ref[index, start + count : start + count + half, :64] = rows[:half, 128:]
        ref[index, start + count : start + count + half, 64:] = rows[half:, 128:]


def unpack_into(ref, where, chunk, main, tail):
    _, count, places = CHUNKS[chunk]
    half = count // 2
    for at, row, size in places:
        ref[*where, row : row + size, :128] = main[at : at + size]
        for lo, hi, lane in ((0, half, 0), (half, count, 64)):
            first, last = max(at, lo), min(at + size, hi)
            if first < last:
                ref[*where, row + first - at : row + last - at, 128:] = tail[
                    first - lo : last - lo, lane : lane + 64
                ]


def kernel(
    occ_ref, shift_ref, orb_hbm, pert_hbm, pot_hbm, table_hbm, out,
    table, orb, pert, pot, v, e,
    osend, orecv, psend, precv, orb_halo, v_halo,
    mine, other, crecv, tiles, ya_recv, xsum, xb_recv, xa_recv, ysum, yb_recv, red,
    gsend, grecv, wsend, wrecv, brow, zsend, zrecv, mat,
    load_sem, osem, psem, fsem, csem, ya_sem, xb_sem, xa_sem, yb_sem, gsem, wsem, zsem, sent,
):
    band = lax.axis_index("band")
    space = lax.axis_index("space")
    core = lax.rem(band, 2)
    y = lax.rem(band // 2, 4)
    x_lo = band // 8
    group = 2 * y + x_lo
    up = lax.rem(space + 1, 8)
    down = lax.rem(space + 7, 8)

    def band_of(x, yy, c):
        return x * 8 + yy * 2 + c

    def y_at(k):
        return lax.rem(y + k, 4)

    def part(name, number=0):
        start, _, height, width = WHERE[name]
        return table[start + number * height : start + (number + 1) * height, :width]

    def pair_of(name):
        return part(name, 0), part(name, 1)

    def wait_bytes(ref, sem):
        pltpu.make_async_copy(ref, ref, sem).wait()

    def send(src, dst, send_sem, recv_sem, to_band, to_space):
        pltpu.make_async_remote_copy(
            src_ref=src,
            dst_ref=dst,
            send_sem=send_sem,
            recv_sem=recv_sem,
            device_id=(to_band, to_space),
            device_id_type=MESH,
        ).start()

    loads = []
    for number, (source, target) in enumerate(
        (
            (pert_hbm.at[0, 0:4], pert.at[4:8]),
            (pert_hbm.at[0, 20:24], pert.at[24:28]),
            (orb_hbm.at[0, 0:4], orb.at[4:8]),
            (orb_hbm.at[0, 20:24], orb.at[24:28]),
            (orb_hbm.at[0, 4:20], orb.at[8:24]),
            (pert_hbm.at[0, 4:20], pert.at[8:24]),
            (pot_hbm, pot),
            (table_hbm, table),
        )
    ):
        copy = pltpu.make_async_copy(source, target, load_sem.at[number])
        copy.start()
        loads.append(copy)

    barrier = pltpu.get_barrier_semaphore()
    for k in range(1, 8):
        for c in range(2):
            pl.semaphore_signal(
                barrier,
                inc=1,
                device_id=(band_of(x_lo, y, c), lax.rem(space + k, 8)),
                device_id_type=MESH,
            )
    for k in range(1, 16):
        pl.semaphore_signal(
            barrier, inc=1, device_id=(lax.rem(band + k, 16), space), device_id_type=MESH
        )

    for layer in list(range(0, 8)) + list(range(32, 40)):
        e[layer] = jnp.zeros((NG, NG), F32)
    for layer in (0, 1, 2, 3, 28, 29, 30, 31):
        v[layer] = jnp.zeros((NG, NG), F32)

    delta = 5.5
    shift = jnp.full((1, NG), shift_ref[0], F32)
    theta = shift + 5.5
    ratio = theta / delta
    w0 = 1.0 / ratio
    w1 = 1.0 / (2.0 * ratio - w0)
    w2 = 1.0 / (2.0 * ratio - w1)
    beta1, beta = 2.0 * w1 / delta, 2.0 * w2 / delta
    a_own = w1 * w0 / theta + beta1
    b_own = beta1 / theta
    b_sten = b_own / 10080.0
    q_shift = shift - 1.5 * COEFFS[0]
    g0 = (1.0 - w2 * w0) / theta
    g1 = 1.0 + w2 * w1 + beta / beta1
    beta_sten = beta / 10080.0
    factor = jnp.full((1, NG), occ_ref[0], F32) * (-4.0 / 16.0)

    piece = 4 * core + y
    piece_row = pl.multiple_of(piece * PIECE, 8)
    half_row = pl.multiple_of(lax.rem(piece, 2) * PIECE, 8)
    loads[0].wait()
    loads[1].wait()
    pack_into(psend, 0, pert[24 + piece // 2])
    pack_into(psend, 1, pert[4 + piece // 2])
    loads[2].wait()
    loads[3].wait()

    pl.semaphore_wait(barrier, 29)

    for way, target in ((0, up), (1, down)):
        send(
            psend.at[way, pl.ds(half_row, PIECE)],
            precv.at[way, pl.ds(piece_row, PIECE)],
            sent.at[0], psem.at[way], band, target,
        )
    for way in range(2):
        for layer in range(4):
            pack_into(osend.at[way], layer, orb[(24 if way == 0 else 4) + layer].astype(F32))
    for chunk, (start, count, _) in enumerate(CHUNKS):
        for way, target in ((0, up), (1, down)):
            send(
                osend.at[way, :, start : start + 3 * count // 2],
                orecv.at[way, :, start : start + 3 * count // 2],
                sent.at[1], osem.at[way, chunk], band, target,
            )

    loads[4].wait()
    loads[5].wait()

    def make_v(layer, carry):
        v[layer] = orb[layer].astype(F32) * pert[layer]
        return carry

    lax.fori_loop(4, 28, make_v, 0)
    loads[6].wait()
    loads[7].wait()

    def along_x(ref, layer, rows):
        total = WEIGHTS[0] * (ref[layer - 1, rows] + ref[layer + 1, rows])
        for offset in range(2, 5):
            total += WEIGHTS[offset - 1] * (
                ref[layer - offset, rows] + ref[layer + offset, rows]
            )
        return total

    def make_e(layer, carry):
        value = v[layer + 4]
        high, low = split(value)
        stencil = part("stencil")
        total = along_x(v, layer + 4, slice(None))
        total += dot(high, stencil) + dot(low, stencil)
        total += dot(stencil, high) + dot(stencil, low)
        diagonal = pot[layer] + q_shift
        e[layer + 8] = (a_own - b_own * diagonal) * value + b_sten * total
        return carry

    def fill_own(ref, n, base, chunk):
        rows = slice(64 * chunk, 64 * chunk + 64)
        around = {0: ((184, 192), (0, 72)), 1: ((56, 136),), 2: ((120, 192), (0, 8))}[chunk]
        stencil, window = part("stencil"), part("window")
        window = jnp.concatenate([window, window], axis=1)
        high, low = split(e[pl.ds(base + 4, 4), rows].reshape(256, NG))
        along_z = dot(high, stencil) + dot(low, stencil)
        for i in range(4):
            layer = base + i
            pieces = [e[layer + 4, lo:hi] for lo, hi in around]
            pieces = pieces[0] if len(pieces) == 1 else jnp.concatenate(pieces, axis=0)
            along_y = dot(window, jnp.concatenate(split(pieces), axis=0))
            total = along_x(e, layer + 4, rows) + (along_y + along_z[64 * i : 64 * i + 64])
            diagonal = pot[layer - 4, rows] + q_shift
            solved = (
                g0 * v[layer, rows]
                + (g1 - beta * diagonal) * e[layer + 4, rows]
                + beta_sten * total
            )
            ref[n, i] = factor * orb[layer, rows].astype(F32) * solved

    def density_beyond(layer, chunk):
        rows = slice(64 * chunk, 64 * chunk + 64)
        at = jnp.where(layer < 4, layer, layer - 24)
        return factor * orb_halo[at, rows] * (beta_sten * along_x(e, layer + 4, rows))

    def make_item(n):
        chunk, block = ITEMS[n]

        def fill(ref, c):
            base = jnp.where(c == 0, 12 - 4 * block, 16 + 4 * block)
            if block < 3:
                fill_own(ref, n, base, chunk)
                return

            def body(layer, carry):
                ref[n, layer] = density_beyond(base + layer, chunk)
                return carry

            lax.fori_loop(0, 4, body, 0)

        fill(other, 1 - core)
        send(
            other.at[n], crecv.at[n], sent.at[2], csem.at[n], band_of(x_lo, y, 1 - core), space
        )
        fill(mine, core)

    def add_cores(n):
        wait_bytes(crecv.at[n], csem.at[n])
        high, low = split((mine[n] + crecv[n]).reshape(256, NG))
        table_high, table_low = pair_of("plain")
        last = ((1,), (1,))
        rows = dot(table_high, high, last) + (
            dot(table_low, high, last) + dot(table_high, low, last)
        )
        for slot in range(2):
            tiles[n, slot] = rows[:, 128 * slot : 128 * slot + 128].reshape(4, 2, 24, 128)

    def ya_start(n):
        add_cores(n)
        i = Y_FIRST.index(n)
        for k in (2, 1, 3):
            send(
                tiles.at[n, :, y_at(k)], ya_recv.at[i, k - 1],
                sent.at[3], ya_sem.at[i], band_of(x_lo, y_at(k), core), space,
            )

    def ya_end(n):
        i = Y_FIRST.index(n)
        wait_bytes(ya_recv.at[i], ya_sem.at[i])
        xsum[i] = (tiles[n, :, y] + ya_recv[i, 0]) + (ya_recv[i, 1] + ya_recv[i, 2])
        send(
            xsum.at[i, :, 1 - x_lo], xb_recv.at[i],
            sent.at[4], xb_sem.at[i], band_of(1 - x_lo, y, core), space,
        )

    def xb_end(n):
        i = Y_FIRST.index(n)
        chunk, block = ITEMS[n]
        wait_bytes(xb_recv.at[i], xb_sem.at[i])
        red[chunk, block] = xsum[i, :, x_lo] + xb_recv[i]

    def xa_start(n):
        add_cores(n)
        i = X_FIRST.index(n)
        send(
            tiles.at[n, :, :, 1 - x_lo], xa_recv.at[i],
            sent.at[5], xa_sem.at[i], band_of(1 - x_lo, y, core), space,
        )

    def xa_end(n):
        i = X_FIRST.index(n)
        wait_bytes(xa_recv.at[i], xa_sem.at[i])
        ysum[i] = tiles[n, :, :, x_lo] + xa_recv[i]
        for k in (2, 1, 3):
            send(
                ysum.at[i, :, y_at(k)], yb_recv.at[i, k - 1],
                sent.at[6], yb_sem.at[i], band_of(x_lo, y_at(k), core), space,
            )

    def yb_end(n):
        i = X_FIRST.index(n)
        chunk, block = ITEMS[n]
        wait_bytes(yb_recv.at[i], yb_sem.at[i])
        red[chunk, block] = (ysum[i, :, y] + yb_recv[i, 0]) + (yb_recv[i, 1] + yb_recv[i, 2])

    lax.fori_loop(4, 20, make_e, 0)

    for way in range(2):
        wait_bytes(precv.at[way, :PIECE], psem.at[way])
    for way in range(2):
        for k in (2, 1, 3):
            send(
                precv.at[way, pl.ds(piece_row, PIECE)],
                precv.at[way, pl.ds(piece_row, PIECE)],
                sent.at[7], fsem.at[0], band_of(x_lo, y_at(k), core), space,
            )
    make_item(0)
    make_item(1)
    make_item(2)
    lax.fori_loop(0, 4, make_e, 0)
    lax.fori_loop(20, 24, make_e, 0)
    wait_bytes(precv.at[0, : 6 * PIECE], fsem.at[0])
    core_row = pl.multiple_of(core * 4 * PIECE, 8)
    for way in range(2):
        send(
            precv.at[way, pl.ds(core_row, 4 * PIECE)],
            precv.at[way, pl.ds(core_row, 4 * PIECE)],
            sent.at[8], fsem.at[1], band_of(x_lo, y, 1 - core), space,
        )
    ya_start(0)
    ya_start(1)
    ya_start(2)

    def take_halo(chunk):
        start, count, places = CHUNKS[chunk]
        half = count // 2
        for way in range(2):
            wait_bytes(orecv.at[way, :, start : start + count + half], osem.at[way, chunk])
            for layer in range(4):
                main = orecv[way, layer, start : start + count]
                tail = orecv[way, layer, start + count : start + count + half]
                row = layer * ROWS + start
                unpack_into(orb_halo, (4 * way + layer,), chunk, main, tail)
                main = main * precv[way, row : row + count]
                tail = tail * precv[way, row + count : row + count + half]
                unpack_into(v_halo, (4 * way + layer,), chunk, main, tail)
        for _, row, size in places:
            rows = slice(row, row + size)
            for x in range(4):
                below = WEIGHTS[3] * v_halo[x, rows]
                for layer in range(x + 1, 4):
                    below += WEIGHTS[3 + x - layer] * v_halo[layer, rows]
                e[x + 8, rows] += b_sten * below
                above = WEIGHTS[3] * v_halo[4 + x, rows]
                for layer in range(x):
                    above += WEIGHTS[3 + layer - x] * v_halo[4 + layer, rows]
                e[x + 28, rows] += b_sten * above

    wait_bytes(precv.at[0, : 8 * PIECE], fsem.at[1])
    take_halo(0)
    make_item(3)
    make_item(4)
    ya_start(3)
    make_item(5)
    ya_start(4)
    ya_start(5)
    for n in range(0, 3):
        ya_end(n)
    take_halo(1)
    make_item(6)
    make_item(7)
    ya_start(6)
    make_item(8)
    ya_start(7)
    ya_start(8)
    for n in range(3, 6):
        ya_end(n)
    take_halo(2)
    make_item(9)
    make_item(10)
    xa_start(9)
    make_item(11)
    ya_start(10)
    xa_start(11)
    for n in range(6, 9):
        ya_end(n)
    xa_end(9)
    for n in range(0, 6):
        xb_end(n)

    mine_at = core * 8 + space

    def to_columns(side):
        blocks = slice(2 * side, 2 * side + 2)
        value = jnp.concatenate(
            [red[chunk, blocks].reshape(96, 128) for chunk in range(3)], axis=1
        )
        high, low = split(value)
        for layer in range(2):
            table_high, table_low = pair_of("forward_y%d" % layer)
            columns = dot(high, table_high) + (dot(low, table_high) + dot(high, table_low))
            for j in range(4):
                for half in range(2):
                    gsend[side, pl.ds(half * 8 + 2 * j + layer, 24, stride=16), :] = columns[
                        24 * j : 24 * j + 24, 128 * half : 128 * half + 128
                    ]
        for k in (4, 3, 5, 2, 6, 1, 7, 0):
            for c in range(2):
                if (k, c) != (0, 0):
                    to_space = lax.rem(space + k, 8)
                    to_core = lax.rem(core + c, 2)
                    row = pl.multiple_of(24 * (to_core * 8 + to_space), 8)
                    send(
                        gsend.at[side, pl.ds(row, 24)], grecv.at[side, mine_at],
                        gsem.at[2], gsem.at[side], band_of(x_lo, y, to_core), to_space,
                    )
        grecv[side, mine_at] = gsend[side, pl.ds(pl.multiple_of(24 * mine_at, 8), 24), :]

    ya_end(10)
    xa_end(11)
    for n in (6, 7, 8, 10):
        xb_end(n)
    to_columns(0)
    yb_end(9)
    yb_end(11)
    to_columns(1)

    kx = lax.broadcasted_iota(jnp.int32, (NG, 128), 0)
    lane = lax.broadcasted_iota(jnp.int32, (NG, 128), 1)
    gx = jnp.minimum(kx, NG - kx)
    factors = []
    for unit in range(3):
        number = 3 * mine_at + unit
        kz = 24 * group + number // 2
        gz = jnp.minimum(kz, NG - kz)
        ky = lane + 128 * lax.rem(number, 2)
        gy = jnp.minimum(ky, NG - ky)
        square = (gx * gx + gy * gy + (gz * gz + 1)).astype(F32)
        factors.append((256.0 / float(NG) ** 3) / jnp.sqrt(square))
    coulomb = jnp.concatenate(factors, axis=1)

    for side in range(2):
        wait_bytes(grecv.at[side, :15], gsem.at[side])
    pencil = jnp.concatenate(
        [grecv[:, :, 8 * unit : 8 * unit + 8, :].reshape(256, 128) for unit in range(3)], axis=1
    )
    spectral = dot3_table_left(pair_of("forward_x"), pencil) * coulomb
    restored = dot3_table_left(pair_of("plain"), spectral)
    for unit in range(3):
        wsend[unit] = restored[:, 128 * unit : 128 * unit + 128]

    for third in range(3):
        for k in (4, 3, 5, 2, 6, 1, 7):
            to_space = lax.rem(space + k, 8)
            row = pl.multiple_of(24 * to_space + 8 * third, 8)
            send(
                wsend.at[:, pl.ds(row, 8)], wrecv.at[third, pl.ds(3 * space, 3)],
                wsem.at[3], wsem.at[third], band, to_space,
            )
    for third in range(3):
        own_row = pl.multiple_of(24 * space + 8 * third, 8)
        wrecv[third, pl.ds(3 * space, 3)] = wsend[:, pl.ds(own_row, 8), :]
    brow[...] = jnp.zeros(brow.shape, F32)
    for third in range(3):
        wait_bytes(wrecv.at[third, :21], wsem.at[third])
        for unit in range(24):
            brow[unit % 2, pl.ds(128 * third + unit // 2, 8, stride=16), :] = wrecv[third, unit]
        rows = jnp.concatenate(
            [brow[half, 128 * third : 128 * third + 128] for half in range(2)], axis=1
        )
        zsend[third] = dot3_table_left(pair_of("inverse_y"), rows, ((1,), (1,)))
        for k in (4, 12, 8, 3, 5, 11, 13, 2, 6, 10, 14, 7, 9, 1, 15):
            to = lax.rem(band + k, 16)
            send(
                zsend.at[third, pl.ds(pl.multiple_of(16 * to, 8), 16)], zrecv.at[third, band],
                zsem.at[3], zsem.at[third], to, space,
            )
        zrecv[third, band] = zsend[third, pl.ds(pl.multiple_of(16 * band, 8), 16), :]

    granule = lax.broadcasted_iota(jnp.int32, (16, 128), 1) // 16
    for third in range(3):
        wait_bytes(zrecv.at[third, :15], zsem.at[third])
        for side in range(2):
            blocks = [zrecv[third, 8 * side + i] for i in range(8)]
            for bit in (1, 2, 4):
                upper = lax.rem(granule // bit, 2) == 1
                after = list(blocks)
                for i in range(8):
                    if not i & bit:
                        low, high = blocks[i], blocks[i | bit]
                        after[i] = jnp.where(upper, pltpu.roll(high, 16 * bit, 1), low)
                        after[i | bit] = jnp.where(upper, high, pltpu.roll(low, 128 - 16 * bit, 1))
                blocks = after
            for i in range(8):
                mat[side, pl.ds(i, 16, stride=8), :] = blocks[i]
        rows = jnp.concatenate([mat[0, :96], mat[1, :96]], axis=1)
        result = dot3_table_right(rows, pair_of("inverse_z"))
        out[0, :, 8 * third : 8 * third + 8] = result.reshape(12, 8, NG)

    wait_bytes(psend.at[:, :PIECE], sent.at[0])
    wait_bytes(osend, sent.at[1])
    wait_bytes(other, sent.at[2])
    wait_bytes(ya_recv, sent.at[3])
    wait_bytes(xb_recv, sent.at[4])
    wait_bytes(xa_recv, sent.at[5])
    wait_bytes(yb_recv, sent.at[6])
    wait_bytes(precv.at[0, : 6 * PIECE], sent.at[7])
    wait_bytes(precv.at[0, : 8 * PIECE], sent.at[8])
    wait_bytes(grecv.at[:, :15], gsem.at[2])
    wait_bytes(wrecv.at[:, :21], wsem.at[3])
    wait_bytes(zrecv.at[:, :15], zsem.at[3])


def on_device(orbitals, occupations, shifts, perturbations, local_potential):
    any_space = pl.BlockSpec(memory_space=pl.ANY)
    smem = pl.BlockSpec(memory_space=pltpu.SMEM)
    vmem = pl.BlockSpec(memory_space=pltpu.VMEM)
    dma = pltpu.SemaphoreType.DMA
    response = pl.pallas_call(
        kernel,
        out_shape=jax.ShapeDtypeStruct((1, 12, SLAB, NG), F32),
        in_specs=[smem] * 2 + [any_space] * 4,
        out_specs=vmem,
        scratch_shapes=[
            pltpu.VMEM(TABLE.shape, BF16),
            pltpu.VMEM((EXT, NG, NG), BF16),
            pltpu.VMEM((EXT, NG, NG), F32),
            pltpu.VMEM((SLAB, NG, NG), F32),
            pltpu.VMEM((EXT, NG, NG), F32),
            pltpu.VMEM((EXT + 8, NG, NG), F32),
            pltpu.VMEM((2, 4, ROWS, 128), F32),
            pltpu.VMEM((2, 4, ROWS, 128), F32),
            pltpu.VMEM((2, ROWS, 128), F32),
            pltpu.VMEM((2, 4 * ROWS, 128), F32),
            pltpu.VMEM((8, NG, NG), F32),
            pltpu.VMEM((8, NG, NG), F32),
            pltpu.VMEM((12, 4, 64, NG), F32),
            pltpu.VMEM((12, 4, 64, NG), F32),
            pltpu.VMEM((12, 4, 64, NG), F32),
            pltpu.VMEM((12, 2, 4, 2, 24, 128), F32),
            pltpu.VMEM((10, 3, 2, 2, 24, 128), F32),
            pltpu.VMEM((10, 2, 2, 24, 128), F32),
            pltpu.VMEM((10, 2, 24, 128), F32),
            pltpu.VMEM((2, 2, 4, 24, 128), F32),
            pltpu.VMEM((2, 2, 4, 24, 128), F32),
            pltpu.VMEM((2, 3, 2, 24, 128), F32),
            pltpu.VMEM((3, 4, 2, 24, 128), F32),
            pltpu.VMEM((2, 384, 128), F32),
            pltpu.VMEM((2, 16, 24, 128), F32),
            pltpu.VMEM((3, NG, 128), F32),
            pltpu.VMEM((3, 24, 8, 128), F32),
            pltpu.VMEM((2, 384, 128), F32),
            pltpu.VMEM((3, 256, 128), F32),
            pltpu.VMEM((3, 16, 16, 128), F32),
            pltpu.VMEM((2, 128, 128), F32),
            dma((8,)),
            dma((2, 3)),
            dma((2,)),
            dma((2,)),
            dma((12,)),
            dma((10,)),
            dma((10,)),
            dma((2,)),
            dma((2,)),
            dma((3,)),
            dma((4,)),
            dma((4,)),
            dma((9,)),
        ],
        compiler_params=pltpu.CompilerParams(
            collective_id=0, has_side_effects=True, vmem_limit_bytes=60 * 2**20
        ),
        name="response",
    )(occupations, shifts, orbitals, perturbations, local_potential, jnp.asarray(TABLE))
    return jnp.transpose(response, (0, 2, 1, 3))


def solution(mesh):
    in_specs = (
        P("band", "space", None, None),
        P("band"),
        P("band"),
        P(None, "space", None, None),
        P("space", None, None),
    )
    out_specs = P(None, "space", "band", None)
    return jax.shard_map(
        on_device, mesh=mesh, in_specs=in_specs, out_specs=out_specs, check_vma=False
    )
```

```python
import math

import jax
import jax.numpy as jnp
import numpy as np
from jax import lax
from jax.experimental import pallas as pl
from jax.experimental.pallas import tpu as pltpu
from jax.sharding import PartitionSpec as P

MESH = pl.DeviceIdType.MESH
BF16 = jnp.bfloat16
F32 = jnp.float32
NG = 192
SLAB = 24
EXT = 32
COEFFS = (-205.0 / 72.0, 8.0 / 5.0, -1.0 / 5.0, 8.0 / 315.0, -1.0 / 560.0)
WEIGHTS = (8064.0, -1008.0, 128.0, -9.0)
ROWS = 288
PIECE = 4 * ROWS // 8
CHUNKS = (
    (0, 80, ((0, 184, 8), (8, 0, 72))),
    (120, 64, ((0, 72, 64),)),
    (216, 48, ((0, 136, 48),)),
)
ITEMS = ((0, 0), (1, 0), (2, 0), (0, 1), (0, 2), (0, 3), (1, 1), (1, 2), (1, 3), (2, 3), (2, 1), (2, 2))
X_FIRST = (9, 11)
Y_FIRST = tuple(n for n in range(12) if n not in X_FIRST)


def cas(product):
    angles = (np.asarray(product, np.int64) % NG).astype(np.float64) * (2.0 * math.pi / NG)
    return np.cos(angles) + np.sin(angles)


def halves(table):
    table = np.asarray(table, np.float32)
    high = table.astype(jnp.bfloat16)
    low = (table - high.astype(np.float32)).astype(jnp.bfloat16)
    return np.stack([high, low])


def tables():
    index = np.arange(NG)
    plain = cas(index[:, None] * index[None, :])
    stencil = np.zeros((NG, NG), np.float32)
    for offset, weight in enumerate(WEIGHTS, 1):
        for sign in (1, -1):
            stencil[index, (index + sign * offset) % NG] += weight
    window = np.zeros((64, 80), np.float32)
    for offset, weight in enumerate(WEIGHTS, 1):
        for sign in (1, -1):
            window[np.arange(64), np.arange(64) + 8 + sign * offset] += weight
    forward_y = np.zeros((2, 384, 256))
    for layer in range(2):
        for chunk in range(3):
            first = 128 * chunk + 64 * layer
            forward_y[layer, first : first + 64, :NG] = plain[64 * chunk : 64 * chunk + 64]
    forward_x = np.zeros((NG, 256))
    for core in range(2):
        for space in range(8):
            for slot in range(16):
                block, layer = divmod(slot, 4)
                ext = (12 - 4 * block if core == 0 else 16 + 4 * block) + layer
                x = (SLAB * space + ext - 4) % NG
                column = 128 * (slot // 8) + (core * 8 + space) * 8 + slot % 8
                forward_x[:, column] = plain[:, x]
    inverse_y = np.zeros((NG, 256))
    inverse_y[:, :NG] = plain
    inverse_z = np.zeros((256, NG))
    for band in range(16):
        x_lo, y, core = band // 8, (band // 2) % 4, band % 2
        first = 24 * (2 * y + x_lo) + 12 * core
        inverse_z[band * 16 : band * 16 + 12] = plain[first : first + 12]
    pieces = {
        "stencil": stencil.astype(jnp.bfloat16)[None],
        "window": window.astype(jnp.bfloat16)[None],
        "plain": halves(plain),
        "forward_y0": halves(forward_y[0]),
        "forward_y1": halves(forward_y[1]),
        "forward_x": halves(forward_x),
        "inverse_y": halves(inverse_y),
        "inverse_z": halves(inverse_z),
    }
    where, rows, start = {}, [], 0
    for name, piece in pieces.items():
        count, height, width = piece.shape
        where[name] = (start, count, height, width)
        flat = piece.reshape(count * height, width)
        rows.append(np.pad(flat, ((0, 0), (0, 256 - width))))
        start += count * height
    return where, np.concatenate(rows)


WHERE, TABLE = tables()


def split(value):
    high = value.astype(BF16)
    low = (value - high.astype(F32)).astype(BF16)
    return high, low


def dot(a, b, dims=((1,), (0,))):
    return lax.dot_general(a, b, (dims, ((), ())), preferred_element_type=F32)


def dot3_table_left(table, value, dims=((1,), (0,))):
    high, low = split(value)
    return dot(table[0], high, dims) + (dot(table[1], high, dims) + dot(table[0], low, dims))


def dot3_table_right(value, table):
    high, low = split(value)
    return dot(high, table[0]) + (dot(low, table[0]) + dot(high, table[1]))


def pack_into(ref, index, layer):
    for start, count, places in CHUNKS:
        rows = [layer[row : row + size] for _, row, size in places]
        rows = rows[0] if len(rows) == 1 else jnp.concatenate(rows, axis=0)
        half = count // 2
        ref[index, start : start + count, :] = rows[:, :128]
        ref[index, start + count : start + count + half, :64] = rows[:half, 128:]
        ref[index, start + count : start + count + half, 64:] = rows[half:, 128:]


def unpack_into(ref, where, chunk, main, tail):
    _, count, places = CHUNKS[chunk]
    half = count // 2
    for at, row, size in places:
        ref[*where, row : row + size, :128] = main[at : at + size]
        for lo, hi, lane in ((0, half, 0), (half, count, 64)):
            first, last = max(at, lo), min(at + size, hi)
            if first < last:
                ref[*where, row + first - at : row + last - at, 128:] = tail[
                    first - lo : last - lo, lane : lane + 64
                ]


def kernel(
    occ_ref, shift_ref, orb_hbm, pert_hbm, pot_hbm, table_hbm, out,
    table, orb, pert, pot, v, e,
    osend, orecv, psend, precv, orb_halo, v_halo,
    mine, other, crecv, tiles, ya_recv, xsum, xb_recv, xa_recv, ysum, yb_recv, red,
    ready, gsend, grecv, wsend, wrecv, brow, zsend, zrecv, mat,
    load_sem, osem, psem, fsem, csem, ya_sem, xb_sem, xa_sem, yb_sem, gsem, wsem, zsem, sent,
):
    band = lax.axis_index("band")
    space = lax.axis_index("space")
    core = lax.rem(band, 2)
    y = lax.rem(band // 2, 4)
    x_lo = band // 8
    group = 2 * y + x_lo
    up = lax.rem(space + 1, 8)
    down = lax.rem(space + 7, 8)

    def band_of(x, yy, c):
        return x * 8 + yy * 2 + c

    def y_at(k):
        return lax.rem(y + k, 4)

    def part(name, number=0):
        start, _, height, width = WHERE[name]
        return table[start + number * height : start + (number + 1) * height, :width]

    def pair_of(name):
        return part(name, 0), part(name, 1)

    def wait_bytes(ref, sem):
        pltpu.make_async_copy(ref, ref, sem).wait()

    def send(src, dst, send_sem, recv_sem, to_band, to_space):
        pltpu.make_async_remote_copy(
            src_ref=src,
            dst_ref=dst,
            send_sem=send_sem,
            recv_sem=recv_sem,
            device_id=(to_band, to_space),
            device_id_type=MESH,
        ).start()

    loads = []
    for number, (source, target) in enumerate(
        (
            (pert_hbm.at[0, 0:4], pert.at[4:8]),
            (pert_hbm.at[0, 20:24], pert.at[24:28]),
            (orb_hbm.at[0, 0:4], orb.at[4:8]),
            (orb_hbm.at[0, 20:24], orb.at[24:28]),
            (orb_hbm.at[0, 4:20], orb.at[8:24]),
            (pert_hbm.at[0, 4:20], pert.at[8:24]),
            (pot_hbm, pot),
            (table_hbm, table),
        )
    ):
        copy = pltpu.make_async_copy(source, target, load_sem.at[number])
        copy.start()
        loads.append(copy)

    barrier = pltpu.get_barrier_semaphore()
    for k in range(1, 8):
        for c in range(2):
            pl.semaphore_signal(
                barrier,
                inc=1,
                device_id=(band_of(x_lo, y, c), lax.rem(space + k, 8)),
                device_id_type=MESH,
            )
    for k in range(1, 16):
        pl.semaphore_signal(
            barrier, inc=1, device_id=(lax.rem(band + k, 16), space), device_id_type=MESH
        )

    for layer in list(range(0, 8)) + list(range(32, 40)):
        e[layer] = jnp.zeros((NG, NG), F32)
    for layer in (0, 1, 2, 3, 28, 29, 30, 31):
        v[layer] = jnp.zeros((NG, NG), F32)

    delta = 5.5
    shift = jnp.full((1, NG), shift_ref[0], F32)
    theta = shift + 5.5
    ratio = theta / delta
    w0 = 1.0 / ratio
    w1 = 1.0 / (2.0 * ratio - w0)
    w2 = 1.0 / (2.0 * ratio - w1)
    beta1, beta = 2.0 * w1 / delta, 2.0 * w2 / delta
    a_own = w1 * w0 / theta + beta1
    b_own = beta1 / theta
    b_sten = b_own / 10080.0
    q_shift = shift - 1.5 * COEFFS[0]
    g0 = (1.0 - w2 * w0) / theta
    g1 = 1.0 + w2 * w1 + beta / beta1
    beta_sten = beta / 10080.0
    factor = jnp.full((1, NG), occ_ref[0], F32) * (-4.0 / 16.0)

    piece = 4 * core + y
    piece_row = pl.multiple_of(piece * PIECE, 8)
    half_row = pl.multiple_of(lax.rem(piece, 2) * PIECE, 8)
    loads[0].wait()
    loads[1].wait()
    pack_into(psend, 0, pert[24 + piece // 2])
    pack_into(psend, 1, pert[4 + piece // 2])
    loads[2].wait()
    loads[3].wait()

    pl.semaphore_wait(barrier, 29)

    for way, target in ((0, up), (1, down)):
        send(
            psend.at[way, pl.ds(half_row, PIECE)],
            precv.at[way, pl.ds(piece_row, PIECE)],
            sent.at[0], psem.at[way], band, target,
        )
    for way in range(2):
        for layer in range(4):
            pack_into(osend.at[way], layer, orb[(24 if way == 0 else 4) + layer].astype(F32))
    for chunk, (start, count, _) in enumerate(CHUNKS):
        for way, target in ((0, up), (1, down)):
            send(
                osend.at[way, :, start : start + 3 * count // 2],
                orecv.at[way, :, start : start + 3 * count // 2],
                sent.at[1], osem.at[way, chunk], band, target,
            )

    loads[4].wait()
    loads[5].wait()

    def make_v(layer, carry):
        v[layer] = orb[layer].astype(F32) * pert[layer]
        return carry

    lax.fori_loop(4, 28, make_v, 0)
    loads[6].wait()
    loads[7].wait()

    def along_x(ref, layer, rows):
        total = WEIGHTS[0] * (ref[layer - 1, rows] + ref[layer + 1, rows])
        for offset in range(2, 5):
            total += WEIGHTS[offset - 1] * (
                ref[layer - offset, rows] + ref[layer + offset, rows]
            )
        return total

    def make_e(layer, carry):
        value = v[layer + 4]
        high, low = split(value)
        stencil = part("stencil")
        total = along_x(v, layer + 4, slice(None))
        total += dot(high, stencil) + dot(low, stencil)
        total += dot(stencil, high) + dot(stencil, low)
        diagonal = pot[layer] + q_shift
        e[layer + 8] = (a_own - b_own * diagonal) * value + b_sten * total
        return carry

    def in_plane(base, chunk):
        rows = slice(64 * chunk, 64 * chunk + 64)
        around = {0: ((184, 192), (0, 72)), 1: ((56, 136),), 2: ((120, 192), (0, 8))}[chunk]
        stencil, window = part("stencil"), part("window")
        window = jnp.concatenate([window, window], axis=1)
        high, low = split(e[pl.ds(base + 4, 4), rows].reshape(256, NG))
        along_z = dot(high, stencil) + dot(low, stencil)
        totals = []
        for i in range(4):
            pieces = [e[base + i + 4, lo:hi] for lo, hi in around]
            pieces = pieces[0] if len(pieces) == 1 else jnp.concatenate(pieces, axis=0)
            along_y = dot(window, jnp.concatenate(split(pieces), axis=0))
            totals.append(along_y + along_z[64 * i : 64 * i + 64])
        return totals

    def fill_own(ref, n, base, chunk, totals):
        rows = slice(64 * chunk, 64 * chunk + 64)
        for i in range(4):
            layer = base + i
            total = along_x(e, layer + 4, rows) + totals[i]
            diagonal = pot[layer - 4, rows] + q_shift
            solved = (
                g0 * v[layer, rows]
                + (g1 - beta * diagonal) * e[layer + 4, rows]
                + beta_sten * total
            )
            ref[n, i] = factor * orb[layer, rows].astype(F32) * solved

    def base_of(c, block):
        return jnp.where(c == 0, 12 - 4 * block, 16 + 4 * block)

    def prepare(n):
        chunk, block = ITEMS[n]
        for which, c in ((0, 1 - core), (1, core)):
            for i, total in enumerate(in_plane(base_of(c, block), chunk)):
                ready[which, i] = total

    def density_beyond(layer, chunk):
        rows = slice(64 * chunk, 64 * chunk + 64)
        at = jnp.where(layer < 4, layer, layer - 24)
        return factor * orb_halo[at, rows] * (beta_sten * along_x(e, layer + 4, rows))

    def make_item(n):
        chunk, block = ITEMS[n]

        def fill(ref, c):
            base = base_of(c, block)
            if block < 3:
                if n == 10:
                    which = 0 if ref is other else 1
                    totals = [ready[which, i] for i in range(4)]
                else:
                    totals = in_plane(base, chunk)
                fill_own(ref, n, base, chunk, totals)
                return

            def body(layer, carry):
                ref[n, layer] = density_beyond(base + layer, chunk)
                return carry

            lax.fori_loop(0, 4, body, 0)

        fill(other, 1 - core)
        send(
            other.at[n], crecv.at[n], sent.at[2], csem.at[n], band_of(x_lo, y, 1 - core), space
        )
        fill(mine, core)

    def add_cores(n):
        wait_bytes(crecv.at[n], csem.at[n])
        high, low = split((mine[n] + crecv[n]).reshape(256, NG))
        table_high, table_low = pair_of("plain")
        last = ((1,), (1,))
        rows = dot(table_high, high, last) + (
            dot(table_low, high, last) + dot(table_high, low, last)
        )
        for slot in range(2):
            tiles[n, slot] = rows[:, 128 * slot : 128 * slot + 128].reshape(4, 2, 24, 128)

    def ya_start(n):
        add_cores(n)
        i = Y_FIRST.index(n)
        for k in (2, 1, 3):
            send(
                tiles.at[n, :, y_at(k)], ya_recv.at[i, k - 1],
                sent.at[3], ya_sem.at[i], band_of(x_lo, y_at(k), core), space,
            )

    def ya_end(n):
        i = Y_FIRST.index(n)
        wait_bytes(ya_recv.at[i], ya_sem.at[i])
        xsum[i] = (tiles[n, :, y] + ya_recv[i, 0]) + (ya_recv[i, 1] + ya_recv[i, 2])
        send(
            xsum.at[i, :, 1 - x_lo], xb_recv.at[i],
            sent.at[4], xb_sem.at[i], band_of(1 - x_lo, y, core), space,
        )

    def xb_end(n):
        i = Y_FIRST.index(n)
        chunk, block = ITEMS[n]
        wait_bytes(xb_recv.at[i], xb_sem.at[i])
        red[chunk, block] = xsum[i, :, x_lo] + xb_recv[i]

    def xa_start(n):
        add_cores(n)
        i = X_FIRST.index(n)
        send(
            tiles.at[n, :, :, 1 - x_lo], xa_recv.at[i],
            sent.at[5], xa_sem.at[i], band_of(1 - x_lo, y, core), space,
        )

    def xa_end(n):
        i = X_FIRST.index(n)
        wait_bytes(xa_recv.at[i], xa_sem.at[i])
        ysum[i] = tiles[n, :, :, x_lo] + xa_recv[i]
        for k in (2, 1, 3):
            send(
                ysum.at[i, :, y_at(k)], yb_recv.at[i, k - 1],
                sent.at[6], yb_sem.at[i], band_of(x_lo, y_at(k), core), space,
            )

    def yb_end(n):
        i = X_FIRST.index(n)
        chunk, block = ITEMS[n]
        wait_bytes(yb_recv.at[i], yb_sem.at[i])
        red[chunk, block] = (ysum[i, :, y] + yb_recv[i, 0]) + (yb_recv[i, 1] + yb_recv[i, 2])

    lax.fori_loop(4, 20, make_e, 0)

    for way in range(2):
        wait_bytes(precv.at[way, :PIECE], psem.at[way])
    for way in range(2):
        for k in (2, 1, 3):
            send(
                precv.at[way, pl.ds(piece_row, PIECE)],
                precv.at[way, pl.ds(piece_row, PIECE)],
                sent.at[7], fsem.at[0], band_of(x_lo, y_at(k), core), space,
            )
    make_item(0)
    make_item(1)
    make_item(2)
    lax.fori_loop(0, 4, make_e, 0)
    lax.fori_loop(20, 24, make_e, 0)
    wait_bytes(precv.at[0, : 6 * PIECE], fsem.at[0])
    core_row = pl.multiple_of(core * 4 * PIECE, 8)
    for way in range(2):
        send(
            precv.at[way, pl.ds(core_row, 4 * PIECE)],
            precv.at[way, pl.ds(core_row, 4 * PIECE)],
            sent.at[8], fsem.at[1], band_of(x_lo, y, 1 - core), space,
        )
    ya_start(0)
    ya_start(1)
    ya_start(2)

    def take_halo(chunk):
        start, count, places = CHUNKS[chunk]
        half = count // 2
        for way in range(2):
            wait_bytes(orecv.at[way, :, start : start + count + half], osem.at[way, chunk])
            for layer in range(4):
                main = orecv[way, layer, start : start + count]
                tail = orecv[way, layer, start + count : start + count + half]
                row = layer * ROWS + start
                unpack_into(orb_halo, (4 * way + layer,), chunk, main, tail)
                main = main * precv[way, row : row + count]
                tail = tail * precv[way, row + count : row + count + half]
                unpack_into(v_halo, (4 * way + layer,), chunk, main, tail)
        for _, row, size in places:
            rows = slice(row, row + size)
            for x in range(4):
                below = WEIGHTS[3] * v_halo[x, rows]
                for layer in range(x + 1, 4):
                    below += WEIGHTS[3 + x - layer] * v_halo[layer, rows]
                e[x + 8, rows] += b_sten * below
                above = WEIGHTS[3] * v_halo[4 + x, rows]
                for layer in range(x):
                    above += WEIGHTS[3 + layer - x] * v_halo[4 + layer, rows]
                e[x + 28, rows] += b_sten * above

    wait_bytes(precv.at[0, : 8 * PIECE], fsem.at[1])
    take_halo(0)
    make_item(3)
    make_item(4)
    ya_start(3)
    make_item(5)
    ya_start(4)
    ya_start(5)
    for n in range(0, 3):
        ya_end(n)
    take_halo(1)
    make_item(6)
    make_item(7)
    ya_start(6)
    make_item(8)
    ya_start(7)
    ya_start(8)
    prepare(10)
    for n in range(3, 6):
        ya_end(n)
    take_halo(2)
    make_item(9)
    make_item(10)
    xa_start(9)
    make_item(11)
    ya_start(10)
    xa_start(11)
    for n in range(6, 9):
        ya_end(n)
    xa_end(9)
    for n in range(0, 6):
        xb_end(n)

    mine_at = core * 8 + space

    def to_columns(side):
        blocks = slice(2 * side, 2 * side + 2)
        value = jnp.concatenate(
            [red[chunk, blocks].reshape(96, 128) for chunk in range(3)], axis=1
        )
        high, low = split(value)
        for layer in range(2):
            table_high, table_low = pair_of("forward_y%d" % layer)
            columns = dot(high, table_high) + (dot(low, table_high) + dot(high, table_low))
            for j in range(4):
                for half in range(2):
                    gsend[side, pl.ds(half * 8 + 2 * j + layer, 24, stride=16), :] = columns[
                        24 * j : 24 * j + 24, 128 * half : 128 * half + 128
                    ]
        for k in (3, 5, 1, 7, 4, 2, 6, 0):
            for c in range(2):
                if (k, c) != (0, 0):
                    to_space = lax.rem(space + k, 8)
                    to_core = lax.rem(core + c, 2)
                    row = pl.multiple_of(24 * (to_core * 8 + to_space), 8)
                    send(
                        gsend.at[side, pl.ds(row, 24)], grecv.at[side, mine_at],
                        gsem.at[2], gsem.at[side], band_of(x_lo, y, to_core), to_space,
                    )
        grecv[side, mine_at] = gsend[side, pl.ds(pl.multiple_of(24 * mine_at, 8), 24), :]

    ya_end(10)
    xa_end(11)
    for n in (6, 7, 8, 10):
        xb_end(n)
    to_columns(0)
    yb_end(9)
    yb_end(11)
    to_columns(1)

    kx = lax.broadcasted_iota(jnp.int32, (NG, 128), 0)
    lane = lax.broadcasted_iota(jnp.int32, (NG, 128), 1)
    gx = jnp.minimum(kx, NG - kx)
    factors = []
    for unit in range(3):
        number = 3 * mine_at + unit
        kz = 24 * group + number // 2
        gz = jnp.minimum(kz, NG - kz)
        ky = lane + 128 * lax.rem(number, 2)
        gy = jnp.minimum(ky, NG - ky)
        square = (gx * gx + gy * gy + (gz * gz + 1)).astype(F32)
        factors.append((256.0 / float(NG) ** 3) / jnp.sqrt(square))
    coulomb = jnp.concatenate(factors, axis=1)

    for side in range(2):
        wait_bytes(grecv.at[side, :15], gsem.at[side])
    pencil = jnp.concatenate(
        [grecv[:, :, 8 * unit : 8 * unit + 8, :].reshape(256, 128) for unit in range(3)], axis=1
    )
    spectral = dot3_table_left(pair_of("forward_x"), pencil) * coulomb
    restored = dot3_table_left(pair_of("plain"), spectral)
    for unit in range(3):
        wsend[unit] = restored[:, 128 * unit : 128 * unit + 128]

    for third in range(3):
        for k in (3, 5, 1, 7, 4, 2, 6):
            to_space = lax.rem(space + k, 8)
            row = pl.multiple_of(24 * to_space + 8 * third, 8)
            send(
                wsend.at[:, pl.ds(row, 8)], wrecv.at[third, pl.ds(3 * space, 3)],
                wsem.at[3], wsem.at[third], band, to_space,
            )
    for third in range(3):
        own_row = pl.multiple_of(24 * space + 8 * third, 8)
        wrecv[third, pl.ds(3 * space, 3)] = wsend[:, pl.ds(own_row, 8), :]
    brow[...] = jnp.zeros(brow.shape, F32)
    for third in range(3):
        wait_bytes(wrecv.at[third, :21], wsem.at[third])
        for unit in range(24):
            brow[unit % 2, pl.ds(128 * third + unit // 2, 8, stride=16), :] = wrecv[third, unit]
        rows = jnp.concatenate(
            [brow[half, 128 * third : 128 * third + 128] for half in range(2)], axis=1
        )
        zsend[third] = dot3_table_left(pair_of("inverse_y"), rows, ((1,), (1,))).reshape(48, 4, 128)
        for k in (4, 12, 8, 3, 5, 11, 13, 2, 6, 10, 14, 7, 9, 1, 15):
            to = lax.rem(band + k, 16)
            send(
                zsend.at[third, pl.ds(3 * to, 3)], zrecv.at[third, band],
                zsem.at[3], zsem.at[third], to, space,
            )
        zrecv[third, band] = zsend[third, pl.ds(3 * band, 3)]

    granule = lax.broadcasted_iota(jnp.int32, (12, 128), 1) // 16
    for third in range(3):
        wait_bytes(zrecv.at[third, :15], zsem.at[third])
        for side in range(2):
            blocks = [zrecv[third, 8 * side + i].reshape(12, 128) for i in range(8)]
            for bit in (1, 2, 4):
                upper = lax.rem(granule // bit, 2) == 1
                after = list(blocks)
                for i in range(8):
                    if not i & bit:
                        low, high = blocks[i], blocks[i | bit]
                        after[i] = jnp.where(upper, pltpu.roll(high, 16 * bit, 1), low)
                        after[i | bit] = jnp.where(upper, high, pltpu.roll(low, 128 - 16 * bit, 1))
                blocks = after
            for i in range(8):
                mat[side, pl.ds(i, 12, stride=8), :] = blocks[i]
        rows = jnp.concatenate([mat[0], mat[1]], axis=1)
        result = dot3_table_right(rows, pair_of("inverse_z"))
        out[0, :, 8 * third : 8 * third + 8] = result.reshape(12, 8, NG)

    wait_bytes(psend.at[:, :PIECE], sent.at[0])
    wait_bytes(osend, sent.at[1])
    wait_bytes(other, sent.at[2])
    wait_bytes(ya_recv, sent.at[3])
    wait_bytes(xb_recv, sent.at[4])
    wait_bytes(xa_recv, sent.at[5])
    wait_bytes(yb_recv, sent.at[6])
    wait_bytes(precv.at[0, : 6 * PIECE], sent.at[7])
    wait_bytes(precv.at[0, : 8 * PIECE], sent.at[8])
    wait_bytes(grecv.at[:, :15], gsem.at[2])
    wait_bytes(wrecv.at[:, :21], wsem.at[3])
    wait_bytes(zrecv.at[:, :15], zsem.at[3])


def on_device(orbitals, occupations, shifts, perturbations, local_potential):
    any_space = pl.BlockSpec(memory_space=pl.ANY)
    smem = pl.BlockSpec(memory_space=pltpu.SMEM)
    vmem = pl.BlockSpec(memory_space=pltpu.VMEM)
    dma = pltpu.SemaphoreType.DMA
    response = pl.pallas_call(
        kernel,
        out_shape=jax.ShapeDtypeStruct((1, 12, SLAB, NG), F32),
        in_specs=[smem] * 2 + [any_space] * 4,
        out_specs=vmem,
        scratch_shapes=[
            pltpu.VMEM(TABLE.shape, BF16),
            pltpu.VMEM((EXT, NG, NG), BF16),
            pltpu.VMEM((EXT, NG, NG), F32),
            pltpu.VMEM((SLAB, NG, NG), F32),
            pltpu.VMEM((EXT, NG, NG), F32),
            pltpu.VMEM((EXT + 8, NG, NG), F32),
            pltpu.VMEM((2, 4, ROWS, 128), F32),
            pltpu.VMEM((2, 4, ROWS, 128), F32),
            pltpu.VMEM((2, ROWS, 128), F32),
            pltpu.VMEM((2, 4 * ROWS, 128), F32),
            pltpu.VMEM((8, NG, NG), F32),
            pltpu.VMEM((8, NG, NG), F32),
            pltpu.VMEM((12, 4, 64, NG), F32),
            pltpu.VMEM((12, 4, 64, NG), F32),
            pltpu.VMEM((12, 4, 64, NG), F32),
            pltpu.VMEM((12, 2, 4, 2, 24, 128), F32),
            pltpu.VMEM((10, 3, 2, 2, 24, 128), F32),
            pltpu.VMEM((10, 2, 2, 24, 128), F32),
            pltpu.VMEM((10, 2, 24, 128), F32),
            pltpu.VMEM((2, 2, 4, 24, 128), F32),
            pltpu.VMEM((2, 2, 4, 24, 128), F32),
            pltpu.VMEM((2, 3, 2, 24, 128), F32),
            pltpu.VMEM((3, 4, 2, 24, 128), F32),
            pltpu.VMEM((2, 4, 64, NG), F32),
            pltpu.VMEM((2, 384, 128), F32),
            pltpu.VMEM((2, 16, 24, 128), F32),
            pltpu.VMEM((3, NG, 128), F32),
            pltpu.VMEM((3, 24, 8, 128), F32),
            pltpu.VMEM((2, 384, 128), F32),
            pltpu.VMEM((3, 48, 4, 128), F32),
            pltpu.VMEM((3, 16, 3, 4, 128), F32),
            pltpu.VMEM((2, 96, 128), F32),
            dma((8,)),
            dma((2, 3)),
            dma((2,)),
            dma((2,)),
            dma((12,)),
            dma((10,)),
            dma((10,)),
            dma((2,)),
            dma((2,)),
            dma((3,)),
            dma((4,)),
            dma((4,)),
            dma((9,)),
        ],
        compiler_params=pltpu.CompilerParams(
            collective_id=0, has_side_effects=True, vmem_limit_bytes=60 * 2**20
        ),
        name="response",
    )(occupations, shifts, orbitals, perturbations, local_potential, jnp.asarray(TABLE))
    return jnp.transpose(response, (0, 2, 1, 3))


def solution(mesh):
    in_specs = (
        P("band", "space", None, None),
        P("band"),
        P("band"),
        P(None, "space", None, None),
        P("space", None, None),
    )
    out_specs = P(None, "space", "band", None)
    return jax.shard_map(
        on_device, mesh=mesh, in_specs=in_specs, out_specs=out_specs, check_vma=False
    )
```

```python
import math

import jax
import jax.numpy as jnp
import numpy as np
from jax import lax
from jax.experimental import pallas as pl
from jax.experimental.pallas import tpu as pltpu
from jax.sharding import PartitionSpec as P

MESH = pl.DeviceIdType.MESH
BF16 = jnp.bfloat16
F32 = jnp.float32
NG = 192
SLAB = 24
EXT = 32
COEFFS = (-205.0 / 72.0, 8.0 / 5.0, -1.0 / 5.0, 8.0 / 315.0, -1.0 / 560.0)
WEIGHTS = (8064.0, -1008.0, 128.0, -9.0)
ROWS = 288
PIECE = 4 * ROWS // 8
CHUNKS = (
    (0, 80, ((0, 184, 8), (8, 0, 72))),
    (120, 64, ((0, 72, 64),)),
    (216, 48, ((0, 136, 48),)),
)
ITEMS = ((0, 0), (1, 0), (2, 0), (0, 1), (0, 2), (0, 3), (1, 1), (1, 2), (1, 3), (2, 3), (2, 1), (2, 2))
X_FIRST = (9, 11)
Y_FIRST = tuple(range(9))


def cas(product):
    angles = (np.asarray(product, np.int64) % NG).astype(np.float64) * (2.0 * math.pi / NG)
    return np.cos(angles) + np.sin(angles)


def halves(table):
    table = np.asarray(table, np.float32)
    high = table.astype(jnp.bfloat16)
    low = (table - high.astype(np.float32)).astype(jnp.bfloat16)
    return np.stack([high, low])


def tables():
    index = np.arange(NG)
    plain = cas(index[:, None] * index[None, :])
    stencil = np.zeros((NG, NG), np.float32)
    for offset, weight in enumerate(WEIGHTS, 1):
        for sign in (1, -1):
            stencil[index, (index + sign * offset) % NG] += weight
    window = np.zeros((64, 80), np.float32)
    for offset, weight in enumerate(WEIGHTS, 1):
        for sign in (1, -1):
            window[np.arange(64), np.arange(64) + 8 + sign * offset] += weight
    forward_y = np.zeros((2, 384, 256))
    for layer in range(2):
        for chunk in range(3):
            first = 128 * chunk + 64 * layer
            forward_y[layer, first : first + 64, :NG] = plain[64 * chunk : 64 * chunk + 64]
    forward_x = np.zeros((NG, 256))
    for core in range(2):
        for space in range(8):
            for slot in range(16):
                block, layer = divmod(slot, 4)
                ext = (12 - 4 * block if core == 0 else 16 + 4 * block) + layer
                x = (SLAB * space + ext - 4) % NG
                column = 128 * (slot // 8) + (core * 8 + space) * 8 + slot % 8
                forward_x[:, column] = plain[:, x]
    inverse_y = np.zeros((NG, 256))
    inverse_y[:, :NG] = plain
    inverse_z = np.zeros((256, NG))
    for band in range(16):
        x_lo, y, core = band // 8, (band // 2) % 4, band % 2
        first = 24 * (2 * y + x_lo) + 12 * core
        inverse_z[band * 16 : band * 16 + 12] = plain[first : first + 12]
    pieces = {
        "stencil": stencil.astype(jnp.bfloat16)[None],
        "window": window.astype(jnp.bfloat16)[None],
        "plain": halves(plain),
        "forward_y0": halves(forward_y[0]),
        "forward_y1": halves(forward_y[1]),
        "forward_x": halves(forward_x),
        "inverse_y": halves(inverse_y),
        "inverse_z": halves(inverse_z),
    }
    where, rows, start = {}, [], 0
    for name, piece in pieces.items():
        count, height, width = piece.shape
        where[name] = (start, count, height, width)
        flat = piece.reshape(count * height, width)
        rows.append(np.pad(flat, ((0, 0), (0, 256 - width))))
        start += count * height
    return where, np.concatenate(rows)


WHERE, TABLE = tables()


def split(value):
    high = value.astype(BF16)
    low = (value - high.astype(F32)).astype(BF16)
    return high, low


def dot(a, b, dims=((1,), (0,))):
    return lax.dot_general(a, b, (dims, ((), ())), preferred_element_type=F32)


def dot3_table_left(table, value, dims=((1,), (0,))):
    high, low = split(value)
    return dot(table[0], high, dims) + (dot(table[1], high, dims) + dot(table[0], low, dims))


def dot3_table_right(value, table):
    high, low = split(value)
    return dot(high, table[0]) + (dot(low, table[0]) + dot(high, table[1]))


def pack_into(ref, index, layer):
    for start, count, places in CHUNKS:
        rows = [layer[row : row + size] for _, row, size in places]
        rows = rows[0] if len(rows) == 1 else jnp.concatenate(rows, axis=0)
        half = count // 2
        ref[index, start : start + count, :] = rows[:, :128]
        ref[index, start + count : start + count + half, :64] = rows[:half, 128:]
        ref[index, start + count : start + count + half, 64:] = rows[half:, 128:]


def unpack_into(ref, where, chunk, main, tail):
    _, count, places = CHUNKS[chunk]
    half = count // 2
    for at, row, size in places:
        ref[*where, row : row + size, :128] = main[at : at + size]
        for lo, hi, lane in ((0, half, 0), (half, count, 64)):
            first, last = max(at, lo), min(at + size, hi)
            if first < last:
                ref[*where, row + first - at : row + last - at, 128:] = tail[
                    first - lo : last - lo, lane : lane + 64
                ]


def kernel(
    occ_ref, shift_ref, orb_hbm, pert_hbm, pot_hbm, table_hbm, out,
    table, orb, pert, pot, v, e,
    osend, orecv, psend, precv, orb_halo, v_halo,
    mine, other, crecv, tiles, ya_recv, xsum, xb_recv, xa_recv, ysum, yb_recv, d_recv, red,
    ready, gsend, grecv, wsend, wrecv, brow, zsend, zrecv, mat,
    load_sem, osem, psem, fsem, csem, ya_sem, xb_sem, xa_sem, yb_sem, d_sem, gsem, wsem, zsem, sent,
):
    band = lax.axis_index("band")
    space = lax.axis_index("space")
    core = lax.rem(band, 2)
    y = lax.rem(band // 2, 4)
    x_lo = band // 8
    group = 2 * y + x_lo
    up = lax.rem(space + 1, 8)
    down = lax.rem(space + 7, 8)

    def band_of(x, yy, c):
        return x * 8 + yy * 2 + c

    def y_at(k):
        return lax.rem(y + k, 4)

    def part(name, number=0):
        start, _, height, width = WHERE[name]
        return table[start + number * height : start + (number + 1) * height, :width]

    def pair_of(name):
        return part(name, 0), part(name, 1)

    def wait_bytes(ref, sem):
        pltpu.make_async_copy(ref, ref, sem).wait()

    def send(src, dst, send_sem, recv_sem, to_band, to_space):
        pltpu.make_async_remote_copy(
            src_ref=src,
            dst_ref=dst,
            send_sem=send_sem,
            recv_sem=recv_sem,
            device_id=(to_band, to_space),
            device_id_type=MESH,
        ).start()

    loads = []
    for number, (source, target) in enumerate(
        (
            (pert_hbm.at[0, 0:4], pert.at[4:8]),
            (pert_hbm.at[0, 20:24], pert.at[24:28]),
            (orb_hbm.at[0, 0:4], orb.at[4:8]),
            (orb_hbm.at[0, 20:24], orb.at[24:28]),
            (orb_hbm.at[0, 4:20], orb.at[8:24]),
            (pert_hbm.at[0, 4:20], pert.at[8:24]),
            (pot_hbm, pot),
            (table_hbm, table),
        )
    ):
        copy = pltpu.make_async_copy(source, target, load_sem.at[number])
        copy.start()
        loads.append(copy)

    barrier = pltpu.get_barrier_semaphore()
    for k in range(1, 8):
        for c in range(2):
            pl.semaphore_signal(
                barrier,
                inc=1,
                device_id=(band_of(x_lo, y, c), lax.rem(space + k, 8)),
                device_id_type=MESH,
            )
    for k in range(1, 16):
        pl.semaphore_signal(
            barrier, inc=1, device_id=(lax.rem(band + k, 16), space), device_id_type=MESH
        )

    for layer in list(range(0, 8)) + list(range(32, 40)):
        e[layer] = jnp.zeros((NG, NG), F32)
    for layer in (0, 1, 2, 3, 28, 29, 30, 31):
        v[layer] = jnp.zeros((NG, NG), F32)

    delta = 5.5
    shift = jnp.full((1, NG), shift_ref[0], F32)
    theta = shift + 5.5
    ratio = theta / delta
    w0 = 1.0 / ratio
    w1 = 1.0 / (2.0 * ratio - w0)
    w2 = 1.0 / (2.0 * ratio - w1)
    beta1, beta = 2.0 * w1 / delta, 2.0 * w2 / delta
    a_own = w1 * w0 / theta + beta1
    b_own = beta1 / theta
    b_sten = b_own / 10080.0
    q_shift = shift - 1.5 * COEFFS[0]
    g0 = (1.0 - w2 * w0) / theta
    g1 = 1.0 + w2 * w1 + beta / beta1
    beta_sten = beta / 10080.0
    factor = jnp.full((1, NG), occ_ref[0], F32) * (-4.0 / 16.0)

    piece = 4 * core + y
    piece_row = pl.multiple_of(piece * PIECE, 8)
    half_row = pl.multiple_of(lax.rem(piece, 2) * PIECE, 8)
    loads[0].wait()
    loads[1].wait()
    pack_into(psend, 0, pert[24 + piece // 2])
    pack_into(psend, 1, pert[4 + piece // 2])
    loads[2].wait()
    loads[3].wait()

    pl.semaphore_wait(barrier, 29)

    for way, target in ((0, up), (1, down)):
        send(
            psend.at[way, pl.ds(half_row, PIECE)],
            precv.at[way, pl.ds(piece_row, PIECE)],
            sent.at[0], psem.at[way], band, target,
        )
    for way in range(2):
        for layer in range(4):
            pack_into(osend.at[way], layer, orb[(24 if way == 0 else 4) + layer].astype(F32))
    for chunk, (start, count, _) in enumerate(CHUNKS):
        for way, target in ((0, up), (1, down)):
            send(
                osend.at[way, :, start : start + 3 * count // 2],
                orecv.at[way, :, start : start + 3 * count // 2],
                sent.at[1], osem.at[way, chunk], band, target,
            )

    loads[4].wait()
    loads[5].wait()

    def make_v(layer, carry):
        v[layer] = orb[layer].astype(F32) * pert[layer]
        return carry

    lax.fori_loop(4, 28, make_v, 0)
    loads[6].wait()
    loads[7].wait()

    def along_x(ref, layer, rows):
        total = WEIGHTS[0] * (ref[layer - 1, rows] + ref[layer + 1, rows])
        for offset in range(2, 5):
            total += WEIGHTS[offset - 1] * (
                ref[layer - offset, rows] + ref[layer + offset, rows]
            )
        return total

    def make_e(layer, carry):
        value = v[layer + 4]
        high, low = split(value)
        stencil = part("stencil")
        total = along_x(v, layer + 4, slice(None))
        total += dot(high, stencil) + dot(low, stencil)
        total += dot(stencil, high) + dot(stencil, low)
        diagonal = pot[layer] + q_shift
        e[layer + 8] = (a_own - b_own * diagonal) * value + b_sten * total
        return carry

    def in_plane(base, chunk):
        rows = slice(64 * chunk, 64 * chunk + 64)
        around = {0: ((184, 192), (0, 72)), 1: ((56, 136),), 2: ((120, 192), (0, 8))}[chunk]
        stencil, window = part("stencil"), part("window")
        window = jnp.concatenate([window, window], axis=1)
        high, low = split(e[pl.ds(base + 4, 4), rows].reshape(256, NG))
        along_z = dot(high, stencil) + dot(low, stencil)
        totals = []
        for i in range(4):
            pieces = [e[base + i + 4, lo:hi] for lo, hi in around]
            pieces = pieces[0] if len(pieces) == 1 else jnp.concatenate(pieces, axis=0)
            along_y = dot(window, jnp.concatenate(split(pieces), axis=0))
            totals.append(along_y + along_z[64 * i : 64 * i + 64])
        return totals

    def fill_own(ref, n, base, chunk, totals):
        rows = slice(64 * chunk, 64 * chunk + 64)
        for i in range(4):
            layer = base + i
            total = along_x(e, layer + 4, rows) + totals[i]
            diagonal = pot[layer - 4, rows] + q_shift
            solved = (
                g0 * v[layer, rows]
                + (g1 - beta * diagonal) * e[layer + 4, rows]
                + beta_sten * total
            )
            ref[n, i] = factor * orb[layer, rows].astype(F32) * solved

    def base_of(c, block):
        return jnp.where(c == 0, 12 - 4 * block, 16 + 4 * block)

    def prepare(n):
        chunk, block = ITEMS[n]
        for which, c in ((0, 1 - core), (1, core)):
            for i, total in enumerate(in_plane(base_of(c, block), chunk)):
                ready[which, i] = total

    def density_beyond(layer, chunk):
        rows = slice(64 * chunk, 64 * chunk + 64)
        at = jnp.where(layer < 4, layer, layer - 24)
        return factor * orb_halo[at, rows] * (beta_sten * along_x(e, layer + 4, rows))

    def make_item(n):
        chunk, block = ITEMS[n]

        def fill(ref, c):
            base = base_of(c, block)
            if block < 3:
                if n == 10:
                    which = 0 if ref is other else 1
                    totals = [ready[which, i] for i in range(4)]
                else:
                    totals = in_plane(base, chunk)
                fill_own(ref, n, base, chunk, totals)
                return

            def body(layer, carry):
                ref[n, layer] = density_beyond(base + layer, chunk)
                return carry

            lax.fori_loop(0, 4, body, 0)

        fill(other, 1 - core)
        send(
            other.at[n], crecv.at[n], sent.at[2], csem.at[n], band_of(x_lo, y, 1 - core), space
        )
        fill(mine, core)

    def add_cores(n):
        wait_bytes(crecv.at[n], csem.at[n])
        high, low = split((mine[n] + crecv[n]).reshape(256, NG))
        table_high, table_low = pair_of("plain")
        last = ((1,), (1,))
        rows = dot(table_high, high, last) + (
            dot(table_low, high, last) + dot(table_high, low, last)
        )
        for slot in range(2):
            tiles[n, slot] = rows[:, 128 * slot : 128 * slot + 128].reshape(4, 2, 24, 128)

    def ya_start(n):
        add_cores(n)
        i = Y_FIRST.index(n)
        for k in (2, 1, 3):
            send(
                tiles.at[n, :, y_at(k)], ya_recv.at[i, k - 1],
                sent.at[3], ya_sem.at[i], band_of(x_lo, y_at(k), core), space,
            )

    def ya_end(n):
        i = Y_FIRST.index(n)
        wait_bytes(ya_recv.at[i], ya_sem.at[i])
        xsum[i] = (tiles[n, :, y] + ya_recv[i, 0]) + (ya_recv[i, 1] + ya_recv[i, 2])
        send(
            xsum.at[i, :, 1 - x_lo], xb_recv.at[i],
            sent.at[4], xb_sem.at[i], band_of(1 - x_lo, y, core), space,
        )

    def xb_end(n):
        i = Y_FIRST.index(n)
        chunk, block = ITEMS[n]
        wait_bytes(xb_recv.at[i], xb_sem.at[i])
        red[chunk, block] = xsum[i, :, x_lo] + xb_recv[i]

    def xa_start(n):
        add_cores(n)
        i = X_FIRST.index(n)
        send(
            tiles.at[n, :, :, 1 - x_lo], xa_recv.at[i],
            sent.at[5], xa_sem.at[i], band_of(1 - x_lo, y, core), space,
        )

    def xa_end(n):
        i = X_FIRST.index(n)
        wait_bytes(xa_recv.at[i], xa_sem.at[i])
        ysum[i] = tiles[n, :, :, x_lo] + xa_recv[i]
        for k in (2, 1, 3):
            send(
                ysum.at[i, :, y_at(k)], yb_recv.at[i, k - 1],
                sent.at[6], yb_sem.at[i], band_of(x_lo, y_at(k), core), space,
            )

    def yb_end(n):
        i = X_FIRST.index(n)
        chunk, block = ITEMS[n]
        wait_bytes(yb_recv.at[i], yb_sem.at[i])
        red[chunk, block] = (ysum[i, :, y] + yb_recv[i, 0]) + (yb_recv[i, 1] + yb_recv[i, 2])

    def d_start(n):
        add_cores(n)
        for k in (6, 2, 5, 7, 1, 3, 4):
            x_to = x_lo if k < 4 else 1 - x_lo
            y_to = y_at(k % 4)
            send(
                tiles.at[n, :, y_to, x_to], d_recv.at[k - 1],
                d_sem.at[0], d_sem.at[1], band_of(x_to, y_to, core), space,
            )

    def d_end(n):
        chunk, block = ITEMS[n]
        wait_bytes(d_recv, d_sem.at[1])
        total = tiles[n, :, y, x_lo] + d_recv[0]
        for k in range(1, 7):
            total += d_recv[k]
        red[chunk, block] = total

    lax.fori_loop(4, 20, make_e, 0)

    for way in range(2):
        wait_bytes(precv.at[way, :PIECE], psem.at[way])
    for way in range(2):
        for k in (2, 1, 3):
            send(
                precv.at[way, pl.ds(piece_row, PIECE)],
                precv.at[way, pl.ds(piece_row, PIECE)],
                sent.at[7], fsem.at[0], band_of(x_lo, y_at(k), core), space,
            )
    make_item(0)
    make_item(1)
    make_item(2)
    lax.fori_loop(0, 4, make_e, 0)
    lax.fori_loop(20, 24, make_e, 0)
    wait_bytes(precv.at[0, : 6 * PIECE], fsem.at[0])
    core_row = pl.multiple_of(core * 4 * PIECE, 8)
    for way in range(2):
        send(
            precv.at[way, pl.ds(core_row, 4 * PIECE)],
            precv.at[way, pl.ds(core_row, 4 * PIECE)],
            sent.at[8], fsem.at[1], band_of(x_lo, y, 1 - core), space,
        )
    ya_start(0)
    ya_start(1)
    ya_start(2)

    def take_halo(chunk):
        start, count, places = CHUNKS[chunk]
        half = count // 2
        for way in range(2):
            wait_bytes(orecv.at[way, :, start : start + count + half], osem.at[way, chunk])
            for layer in range(4):
                main = orecv[way, layer, start : start + count]
                tail = orecv[way, layer, start + count : start + count + half]
                row = layer * ROWS + start
                unpack_into(orb_halo, (4 * way + layer,), chunk, main, tail)
                main = main * precv[way, row : row + count]
                tail = tail * precv[way, row + count : row + count + half]
                unpack_into(v_halo, (4 * way + layer,), chunk, main, tail)
        for _, row, size in places:
            rows = slice(row, row + size)
            for x in range(4):
                below = WEIGHTS[3] * v_halo[x, rows]
                for layer in range(x + 1, 4):
                    below += WEIGHTS[3 + x - layer] * v_halo[layer, rows]
                e[x + 8, rows] += b_sten * below
                above = WEIGHTS[3] * v_halo[4 + x, rows]
                for layer in range(x):
                    above += WEIGHTS[3 + layer - x] * v_halo[4 + layer, rows]
                e[x + 28, rows] += b_sten * above

    wait_bytes(precv.at[0, : 8 * PIECE], fsem.at[1])
    take_halo(0)
    make_item(3)
    make_item(4)
    ya_start(3)
    make_item(5)
    ya_start(4)
    ya_start(5)
    for n in range(0, 3):
        ya_end(n)
    take_halo(1)
    make_item(6)
    make_item(7)
    ya_start(6)
    make_item(8)
    ya_start(7)
    ya_start(8)
    prepare(10)
    for n in range(3, 6):
        ya_end(n)
    take_halo(2)
    make_item(9)
    make_item(10)
    xa_start(9)
    make_item(11)
    d_start(10)
    xa_start(11)
    for n in range(6, 9):
        ya_end(n)
    xa_end(9)
    for n in range(0, 6):
        xb_end(n)

    mine_at = core * 8 + space

    def to_columns(side):
        blocks = slice(2 * side, 2 * side + 2)
        value = jnp.concatenate(
            [red[chunk, blocks].reshape(96, 128) for chunk in range(3)], axis=1
        )
        high, low = split(value)
        for layer in range(2):
            table_high, table_low = pair_of("forward_y%d" % layer)
            columns = dot(high, table_high) + (dot(low, table_high) + dot(high, table_low))
            for j in range(4):
                for half in range(2):
                    gsend[side, pl.ds(half * 8 + 2 * j + layer, 24, stride=16), :] = columns[
                        24 * j : 24 * j + 24, 128 * half : 128 * half + 128
                    ]
        for k in (3, 5, 1, 7, 4, 2, 6, 0):
            for c in range(2):
                if (k, c) != (0, 0):
                    to_space = lax.rem(space + k, 8)
                    to_core = lax.rem(core + c, 2)
                    row = pl.multiple_of(24 * (to_core * 8 + to_space), 8)
                    send(
                        gsend.at[side, pl.ds(row, 24)], grecv.at[side, mine_at],
                        gsem.at[2], gsem.at[side], band_of(x_lo, y, to_core), to_space,
                    )
        grecv[side, mine_at] = gsend[side, pl.ds(pl.multiple_of(24 * mine_at, 8), 24), :]

    xb_end(6)
    d_end(10)
    xa_end(11)
    to_columns(0)
    xb_end(7)
    xb_end(8)
    yb_end(9)
    yb_end(11)
    to_columns(1)

    kx = lax.broadcasted_iota(jnp.int32, (NG, 128), 0)
    lane = lax.broadcasted_iota(jnp.int32, (NG, 128), 1)
    gx = jnp.minimum(kx, NG - kx)
    factors = []
    for unit in range(3):
        number = 3 * mine_at + unit
        kz = 24 * group + number // 2
        gz = jnp.minimum(kz, NG - kz)
        ky = lane + 128 * lax.rem(number, 2)
        gy = jnp.minimum(ky, NG - ky)
        square = (gx * gx + gy * gy + (gz * gz + 1)).astype(F32)
        factors.append((256.0 / float(NG) ** 3) / jnp.sqrt(square))
    coulomb = jnp.concatenate(factors, axis=1)

    for side in range(2):
        wait_bytes(grecv.at[side, :15], gsem.at[side])
    pencil = jnp.concatenate(
        [grecv[:, :, 8 * unit : 8 * unit + 8, :].reshape(256, 128) for unit in range(3)], axis=1
    )
    spectral = dot3_table_left(pair_of("forward_x"), pencil) * coulomb
    restored = dot3_table_left(pair_of("plain"), spectral)
    for unit in range(3):
        wsend[unit] = restored[:, 128 * unit : 128 * unit + 128]

    for third in range(3):
        for k in (3, 5, 1, 7, 4, 2, 6):
            to_space = lax.rem(space + k, 8)
            row = pl.multiple_of(24 * to_space + 8 * third, 8)
            send(
                wsend.at[:, pl.ds(row, 8)], wrecv.at[third, pl.ds(3 * space, 3)],
                wsem.at[3], wsem.at[third], band, to_space,
            )
    for third in range(3):
        own_row = pl.multiple_of(24 * space + 8 * third, 8)
        wrecv[third, pl.ds(3 * space, 3)] = wsend[:, pl.ds(own_row, 8), :]
    brow[...] = jnp.zeros(brow.shape, F32)
    for third in range(3):
        wait_bytes(wrecv.at[third, :21], wsem.at[third])
        for unit in range(24):
            brow[unit % 2, pl.ds(128 * third + unit // 2, 8, stride=16), :] = wrecv[third, unit]
        rows = jnp.concatenate(
            [brow[half, 128 * third : 128 * third + 128] for half in range(2)], axis=1
        )
        zsend[third] = dot3_table_left(pair_of("inverse_y"), rows, ((1,), (1,))).reshape(48, 4, 128)
        for k in (4, 12, 8, 3, 5, 11, 13, 2, 6, 10, 14, 7, 9, 1, 15):
            to = lax.rem(band + k, 16)
            send(
                zsend.at[third, pl.ds(3 * to, 3)], zrecv.at[third, band],
                zsem.at[3], zsem.at[third], to, space,
            )
        zrecv[third, band] = zsend[third, pl.ds(3 * band, 3)]

    granule = lax.broadcasted_iota(jnp.int32, (12, 128), 1) // 16
    for third in range(3):
        wait_bytes(zrecv.at[third, :15], zsem.at[third])
        for side in range(2):
            blocks = [zrecv[third, 8 * side + i].reshape(12, 128) for i in range(8)]
            for bit in (1, 2, 4):
                upper = lax.rem(granule // bit, 2) == 1
                after = list(blocks)
                for i in range(8):
                    if not i & bit:
                        low, high = blocks[i], blocks[i | bit]
                        after[i] = jnp.where(upper, pltpu.roll(high, 16 * bit, 1), low)
                        after[i | bit] = jnp.where(upper, high, pltpu.roll(low, 128 - 16 * bit, 1))
                blocks = after
            for i in range(8):
                mat[side, pl.ds(i, 12, stride=8), :] = blocks[i]
        rows = jnp.concatenate([mat[0], mat[1]], axis=1)
        result = dot3_table_right(rows, pair_of("inverse_z"))
        out[0, :, 8 * third : 8 * third + 8] = result.reshape(12, 8, NG)

    wait_bytes(psend.at[:, :PIECE], sent.at[0])
    wait_bytes(osend, sent.at[1])
    wait_bytes(other, sent.at[2])
    wait_bytes(ya_recv, sent.at[3])
    wait_bytes(xb_recv, sent.at[4])
    wait_bytes(xa_recv, sent.at[5])
    wait_bytes(yb_recv, sent.at[6])
    wait_bytes(d_recv, d_sem.at[0])
    wait_bytes(precv.at[0, : 6 * PIECE], sent.at[7])
    wait_bytes(precv.at[0, : 8 * PIECE], sent.at[8])
    wait_bytes(grecv.at[:, :15], gsem.at[2])
    wait_bytes(wrecv.at[:, :21], wsem.at[3])
    wait_bytes(zrecv.at[:, :15], zsem.at[3])


def on_device(orbitals, occupations, shifts, perturbations, local_potential):
    any_space = pl.BlockSpec(memory_space=pl.ANY)
    smem = pl.BlockSpec(memory_space=pltpu.SMEM)
    vmem = pl.BlockSpec(memory_space=pltpu.VMEM)
    dma = pltpu.SemaphoreType.DMA
    response = pl.pallas_call(
        kernel,
        out_shape=jax.ShapeDtypeStruct((1, 12, SLAB, NG), F32),
        in_specs=[smem] * 2 + [any_space] * 4,
        out_specs=vmem,
        scratch_shapes=[
            pltpu.VMEM(TABLE.shape, BF16),
            pltpu.VMEM((EXT, NG, NG), BF16),
            pltpu.VMEM((EXT, NG, NG), F32),
            pltpu.VMEM((SLAB, NG, NG), F32),
            pltpu.VMEM((EXT, NG, NG), F32),
            pltpu.VMEM((EXT + 8, NG, NG), F32),
            pltpu.VMEM((2, 4, ROWS, 128), F32),
            pltpu.VMEM((2, 4, ROWS, 128), F32),
            pltpu.VMEM((2, ROWS, 128), F32),
            pltpu.VMEM((2, 4 * ROWS, 128), F32),
            pltpu.VMEM((8, NG, NG), F32),
            pltpu.VMEM((8, NG, NG), F32),
            pltpu.VMEM((12, 4, 64, NG), F32),
            pltpu.VMEM((12, 4, 64, NG), F32),
            pltpu.VMEM((12, 4, 64, NG), F32),
            pltpu.VMEM((12, 2, 4, 2, 24, 128), F32),
            pltpu.VMEM((9, 3, 2, 2, 24, 128), F32),
            pltpu.VMEM((9, 2, 2, 24, 128), F32),
            pltpu.VMEM((9, 2, 24, 128), F32),
            pltpu.VMEM((2, 2, 4, 24, 128), F32),
            pltpu.VMEM((2, 2, 4, 24, 128), F32),
            pltpu.VMEM((2, 3, 2, 24, 128), F32),
            pltpu.VMEM((7, 2, 24, 128), F32),
            pltpu.VMEM((3, 4, 2, 24, 128), F32),
            pltpu.VMEM((2, 4, 64, NG), F32),
            pltpu.VMEM((2, 384, 128), F32),
            pltpu.VMEM((2, 16, 24, 128), F32),
            pltpu.VMEM((3, NG, 128), F32),
            pltpu.VMEM((3, 24, 8, 128), F32),
            pltpu.VMEM((2, 384, 128), F32),
            pltpu.VMEM((3, 48, 4, 128), F32),
            pltpu.VMEM((3, 16, 3, 4, 128), F32),
            pltpu.VMEM((2, 96, 128), F32),
            dma((8,)),
            dma((2, 3)),
            dma((2,)),
            dma((2,)),
            dma((12,)),
            dma((9,)),
            dma((9,)),
            dma((2,)),
            dma((2,)),
            dma((2,)),
            dma((3,)),
            dma((4,)),
            dma((4,)),
            dma((9,)),
        ],
        compiler_params=pltpu.CompilerParams(
            collective_id=0, has_side_effects=True, vmem_limit_bytes=60 * 2**20
        ),
        name="response",
    )(occupations, shifts, orbitals, perturbations, local_potential, jnp.asarray(TABLE))
    return jnp.transpose(response, (0, 2, 1, 3))


def solution(mesh):
    in_specs = (
        P("band", "space", None, None),
        P("band"),
        P("band"),
        P(None, "space", None, None),
        P("space", None, None),
    )
    out_specs = P(None, "space", "band", None)
    return jax.shard_map(
        on_device, mesh=mesh, in_specs=in_specs, out_specs=out_specs, check_vma=False
    )
```

```python
import math

import jax
import jax.numpy as jnp
import numpy as np
from jax import lax
from jax.experimental import pallas as pl
from jax.experimental.pallas import tpu as pltpu
from jax.sharding import PartitionSpec as P

MESH = pl.DeviceIdType.MESH
BF16 = jnp.bfloat16
F32 = jnp.float32
NG = 192
SLAB = 24
EXT = 32
COEFFS = (-205.0 / 72.0, 8.0 / 5.0, -1.0 / 5.0, 8.0 / 315.0, -1.0 / 560.0)
WEIGHTS = (8064.0, -1008.0, 128.0, -9.0)
ROWS = 288
PIECE = 4 * ROWS // 8
CHUNKS = (
    (0, 80, ((0, 184, 8), (8, 0, 72))),
    (120, 64, ((0, 72, 64),)),
    (216, 48, ((0, 136, 48),)),
)
ITEMS = ((0, 0), (1, 0), (2, 0), (0, 1), (0, 2), (0, 3), (1, 1), (1, 2), (1, 3), (2, 3), (2, 1), (2, 2))
X_FIRST = (9, 11)
Y_FIRST = tuple(n for n in range(12) if n not in X_FIRST)


def cas(product):
    angles = (np.asarray(product, np.int64) % NG).astype(np.float64) * (2.0 * math.pi / NG)
    return np.cos(angles) + np.sin(angles)


def halves(table):
    table = np.asarray(table, np.float32)
    high = table.astype(jnp.bfloat16)
    low = (table - high.astype(np.float32)).astype(jnp.bfloat16)
    return np.stack([high, low])


def tables():
    index = np.arange(NG)
    plain = cas(index[:, None] * index[None, :])
    stencil = np.zeros((NG, NG), np.float32)
    for offset, weight in enumerate(WEIGHTS, 1):
        for sign in (1, -1):
            stencil[index, (index + sign * offset) % NG] += weight
    window = np.zeros((64, 80), np.float32)
    for offset, weight in enumerate(WEIGHTS, 1):
        for sign in (1, -1):
            window[np.arange(64), np.arange(64) + 8 + sign * offset] += weight
    forward_y = np.zeros((2, 384, 256))
    for layer in range(2):
        for chunk in range(3):
            first = 128 * chunk + 64 * layer
            forward_y[layer, first : first + 64, :NG] = plain[64 * chunk : 64 * chunk + 64]
    forward_x = np.zeros((NG, 256))
    for core in range(2):
        for space in range(8):
            for slot in range(16):
                block, layer = divmod(slot, 4)
                ext = (12 - 4 * block if core == 0 else 16 + 4 * block) + layer
                x = (SLAB * space + ext - 4) % NG
                column = 128 * (slot // 8) + (core * 8 + space) * 8 + slot % 8
                forward_x[:, column] = plain[:, x]
    inverse_y = np.zeros((NG, 256))
    inverse_y[:, :NG] = plain
    inverse_z = np.zeros((256, NG))
    for band in range(16):
        x_lo, y, core = band // 8, (band // 2) % 4, band % 2
        first = 24 * (2 * y + x_lo) + 12 * core
        inverse_z[band * 16 : band * 16 + 12] = plain[first : first + 12]
    pieces = {
        "stencil": stencil.astype(jnp.bfloat16)[None],
        "window": window.astype(jnp.bfloat16)[None],
        "plain": halves(plain),
        "forward_y0": halves(forward_y[0]),
        "forward_y1": halves(forward_y[1]),
        "forward_x": halves(forward_x),
        "inverse_y": halves(inverse_y),
        "inverse_z": halves(inverse_z),
    }
    where, rows, start = {}, [], 0
    for name, piece in pieces.items():
        count, height, width = piece.shape
        where[name] = (start, count, height, width)
        flat = piece.reshape(count * height, width)
        rows.append(np.pad(flat, ((0, 0), (0, 256 - width))))
        start += count * height
    return where, np.concatenate(rows)


WHERE, TABLE = tables()


def split(value):
    high = value.astype(BF16)
    low = (value - high.astype(F32)).astype(BF16)
    return high, low


def dot(a, b, dims=((1,), (0,))):
    return lax.dot_general(a, b, (dims, ((), ())), preferred_element_type=F32)


def dot3_table_left(table, value, dims=((1,), (0,))):
    high, low = split(value)
    return dot(table[0], high, dims) + (dot(table[1], high, dims) + dot(table[0], low, dims))


def dot3_table_right(value, table):
    high, low = split(value)
    return dot(high, table[0]) + (dot(low, table[0]) + dot(high, table[1]))


def pack_into(ref, index, layer):
    for start, count, places in CHUNKS:
        rows = [layer[row : row + size] for _, row, size in places]
        rows = rows[0] if len(rows) == 1 else jnp.concatenate(rows, axis=0)
        half = count // 2
        ref[index, start : start + count, :] = rows[:, :128]
        ref[index, start + count : start + count + half, :64] = rows[:half, 128:]
        ref[index, start + count : start + count + half, 64:] = rows[half:, 128:]


def unpack_into(ref, where, chunk, main, tail):
    _, count, places = CHUNKS[chunk]
    half = count // 2
    for at, row, size in places:
        ref[*where, row : row + size, :128] = main[at : at + size]
        for lo, hi, lane in ((0, half, 0), (half, count, 64)):
            first, last = max(at, lo), min(at + size, hi)
            if first < last:
                ref[*where, row + first - at : row + last - at, 128:] = tail[
                    first - lo : last - lo, lane : lane + 64
                ]


def kernel(
    occ_ref, shift_ref, orb_hbm, pert_hbm, pot_hbm, table_hbm, out,
    table, orb, pert, pot, v, e,
    osend, orecv, psend, precv, orb_halo, v_halo,
    mine, other, crecv, tiles, ya_recv, xsum, xb_recv, xa_recv, ysum, yb_recv, red,
    ready, gsend, grecv, wsend, wrecv, brow, zsend, zrecv, mat,
    load_sem, osem, psem, fsem, csem, ya_sem, xb_sem, xa_sem, yb_sem, gsem, wsem, zsem, sent,
):
    band = lax.axis_index("band")
    space = lax.axis_index("space")
    core = lax.rem(band, 2)
    y = lax.rem(band // 2, 4)
    x_lo = band // 8
    group = 2 * y + x_lo
    up = lax.rem(space + 1, 8)
    down = lax.rem(space + 7, 8)

    def band_of(x, yy, c):
        return x * 8 + yy * 2 + c

    def y_at(k):
        return lax.rem(y + k, 4)

    def part(name, number=0):
        start, _, height, width = WHERE[name]
        return table[start + number * height : start + (number + 1) * height, :width]

    def pair_of(name):
        return part(name, 0), part(name, 1)

    def wait_bytes(ref, sem):
        pltpu.make_async_copy(ref, ref, sem).wait()

    def send(src, dst, send_sem, recv_sem, to_band, to_space):
        pltpu.make_async_remote_copy(
            src_ref=src,
            dst_ref=dst,
            send_sem=send_sem,
            recv_sem=recv_sem,
            device_id=(to_band, to_space),
            device_id_type=MESH,
        ).start()

    loads = []
    for number, (source, target) in enumerate(
        (
            (pert_hbm.at[0, 0:4], pert.at[4:8]),
            (pert_hbm.at[0, 20:24], pert.at[24:28]),
            (orb_hbm.at[0, 0:4], orb.at[4:8]),
            (orb_hbm.at[0, 20:24], orb.at[24:28]),
            (orb_hbm.at[0, 4:20], orb.at[8:24]),
            (pert_hbm.at[0, 4:20], pert.at[8:24]),
            (pot_hbm, pot),
            (table_hbm, table),
        )
    ):
        copy = pltpu.make_async_copy(source, target, load_sem.at[number])
        copy.start()
        loads.append(copy)

    barrier = pltpu.get_barrier_semaphore()
    for k in range(1, 8):
        for c in range(2):
            pl.semaphore_signal(
                barrier,
                inc=1,
                device_id=(band_of(x_lo, y, c), lax.rem(space + k, 8)),
                device_id_type=MESH,
            )
    for k in range(1, 16):
        pl.semaphore_signal(
            barrier, inc=1, device_id=(lax.rem(band + k, 16), space), device_id_type=MESH
        )

    for layer in list(range(0, 8)) + list(range(32, 40)):
        e[layer] = jnp.zeros((NG, NG), F32)
    for layer in (0, 1, 2, 3, 28, 29, 30, 31):
        v[layer] = jnp.zeros((NG, NG), F32)

    delta = 5.5
    shift = jnp.full((1, NG), shift_ref[0], F32)
    theta = shift + 5.5
    ratio = theta / delta
    w0 = 1.0 / ratio
    w1 = 1.0 / (2.0 * ratio - w0)
    w2 = 1.0 / (2.0 * ratio - w1)
    beta1, beta = 2.0 * w1 / delta, 2.0 * w2 / delta
    a_own = w1 * w0 / theta + beta1
    b_own = beta1 / theta
    b_sten = b_own / 10080.0
    q_shift = shift - 1.5 * COEFFS[0]
    g0 = (1.0 - w2 * w0) / theta
    g1 = 1.0 + w2 * w1 + beta / beta1
    beta_sten = beta / 10080.0
    factor = jnp.full((1, NG), occ_ref[0], F32) * (-4.0 / 16.0)

    piece = 4 * core + y
    piece_row = pl.multiple_of(piece * PIECE, 8)
    half_row = pl.multiple_of(lax.rem(piece, 2) * PIECE, 8)
    loads[0].wait()
    loads[1].wait()
    pack_into(psend, 0, pert[24 + piece // 2])
    pack_into(psend, 1, pert[4 + piece // 2])
    loads[2].wait()
    loads[3].wait()

    pl.semaphore_wait(barrier, 29)

    for way, target in ((0, up), (1, down)):
        send(
            psend.at[way, pl.ds(half_row, PIECE)],
            precv.at[way, pl.ds(piece_row, PIECE)],
            sent.at[0], psem.at[way], band, target,
        )
    for way in range(2):
        for layer in range(4):
            pack_into(osend.at[way], layer, orb[(24 if way == 0 else 4) + layer].astype(F32))
    for chunk, (start, count, _) in enumerate(CHUNKS):
        for way, target in ((0, up), (1, down)):
            send(
                osend.at[way, :, start : start + 3 * count // 2],
                orecv.at[way, :, start : start + 3 * count // 2],
                sent.at[1], osem.at[way, chunk], band, target,
            )

    loads[4].wait()
    loads[5].wait()

    def make_v(layer, carry):
        v[layer] = orb[layer].astype(F32) * pert[layer]
        return carry

    lax.fori_loop(4, 28, make_v, 0)
    loads[6].wait()
    loads[7].wait()

    def along_x(ref, layer, rows):
        total = WEIGHTS[0] * (ref[layer - 1, rows] + ref[layer + 1, rows])
        for offset in range(2, 5):
            total += WEIGHTS[offset - 1] * (
                ref[layer - offset, rows] + ref[layer + offset, rows]
            )
        return total

    def make_e(layer, carry):
        value = v[layer + 4]
        high, low = split(value)
        stencil = part("stencil")
        total = along_x(v, layer + 4, slice(None))
        total += dot(high, stencil) + dot(low, stencil)
        total += dot(stencil, high) + dot(stencil, low)
        diagonal = pot[layer] + q_shift
        e[layer + 8] = (a_own - b_own * diagonal) * value + b_sten * total
        return carry

    def in_plane(base, chunk):
        rows = slice(64 * chunk, 64 * chunk + 64)
        around = {0: ((184, 192), (0, 72)), 1: ((56, 136),), 2: ((120, 192), (0, 8))}[chunk]
        stencil, window = part("stencil"), part("window")
        window = jnp.concatenate([window, window], axis=1)
        high, low = split(e[pl.ds(base + 4, 4), rows].reshape(256, NG))
        along_z = dot(high, stencil) + dot(low, stencil)
        totals = []
        for i in range(4):
            pieces = [e[base + i + 4, lo:hi] for lo, hi in around]
            pieces = pieces[0] if len(pieces) == 1 else jnp.concatenate(pieces, axis=0)
            along_y = dot(window, jnp.concatenate(split(pieces), axis=0))
            totals.append(along_y + along_z[64 * i : 64 * i + 64])
        return totals

    def fill_own(ref, n, base, chunk, totals):
        rows = slice(64 * chunk, 64 * chunk + 64)
        for i in range(4):
            layer = base + i
            total = along_x(e, layer + 4, rows) + totals[i]
            diagonal = pot[layer - 4, rows] + q_shift
            solved = (
                g0 * v[layer, rows]
                + (g1 - beta * diagonal) * e[layer + 4, rows]
                + beta_sten * total
            )
            ref[n, i] = factor * orb[layer, rows].astype(F32) * solved

    def base_of(c, block):
        return jnp.where(c == 0, 12 - 4 * block, 16 + 4 * block)

    def prepare(n):
        chunk, block = ITEMS[n]
        for which, c in ((0, 1 - core), (1, core)):
            for i, total in enumerate(in_plane(base_of(c, block), chunk)):
                ready[which, i] = total

    def density_beyond(layer, chunk):
        rows = slice(64 * chunk, 64 * chunk + 64)
        at = jnp.where(layer < 4, layer, layer - 24)
        return factor * orb_halo[at, rows] * (beta_sten * along_x(e, layer + 4, rows))

    def make_item(n):
        chunk, block = ITEMS[n]

        def fill(ref, c):
            base = base_of(c, block)
            if block < 3:
                if n == 10:
                    which = 0 if ref is other else 1
                    totals = [ready[which, i] for i in range(4)]
                else:
                    totals = in_plane(base, chunk)
                fill_own(ref, n, base, chunk, totals)
                return

            def body(layer, carry):
                ref[n, layer] = density_beyond(base + layer, chunk)
                return carry

            lax.fori_loop(0, 4, body, 0)

        fill(other, 1 - core)
        send(
            other.at[n], crecv.at[n], sent.at[2], csem.at[n], band_of(x_lo, y, 1 - core), space
        )
        fill(mine, core)

    def add_cores(n):
        wait_bytes(crecv.at[n], csem.at[n])
        high, low = split((mine[n] + crecv[n]).reshape(256, NG))
        table_high, table_low = pair_of("plain")
        last = ((1,), (1,))
        rows = dot(table_high, high, last) + (
            dot(table_low, high, last) + dot(table_high, low, last)
        )
        for slot in range(2):
            tiles[n, slot] = rows[:, 128 * slot : 128 * slot + 128].reshape(4, 2, 24, 128)

    def ya_start(n):
        add_cores(n)
        i = Y_FIRST.index(n)
        for k in (2, 1, 3):
            send(
                tiles.at[n, :, y_at(k)], ya_recv.at[i, k - 1],
                sent.at[3], ya_sem.at[i], band_of(x_lo, y_at(k), core), space,
            )

    def ya_end(n):
        i = Y_FIRST.index(n)
        wait_bytes(ya_recv.at[i], ya_sem.at[i])
        xsum[i] = (tiles[n, :, y] + ya_recv[i, 0]) + (ya_recv[i, 1] + ya_recv[i, 2])
        send(
            xsum.at[i, :, 1 - x_lo], xb_recv.at[i],
            sent.at[4], xb_sem.at[i], band_of(1 - x_lo, y, core), space,
        )

    def xb_end(n):
        i = Y_FIRST.index(n)
        chunk, block = ITEMS[n]
        wait_bytes(xb_recv.at[i], xb_sem.at[i])
        red[chunk, block] = xsum[i, :, x_lo] + xb_recv[i]

    def xa_start(n):
        add_cores(n)
        i = X_FIRST.index(n)
        send(
            tiles.at[n, :, :, 1 - x_lo], xa_recv.at[i],
            sent.at[5], xa_sem.at[i], band_of(1 - x_lo, y, core), space,
        )

    def xa_end(n):
        i = X_FIRST.index(n)
        wait_bytes(xa_recv.at[i], xa_sem.at[i])
        ysum[i] = tiles[n, :, :, x_lo] + xa_recv[i]
        for k in (2, 1, 3):
            send(
                ysum.at[i, :, y_at(k)], yb_recv.at[i, k - 1],
                sent.at[6], yb_sem.at[i], band_of(x_lo, y_at(k), core), space,
            )

    def yb_end(n):
        i = X_FIRST.index(n)
        chunk, block = ITEMS[n]
        wait_bytes(yb_recv.at[i], yb_sem.at[i])
        red[chunk, block] = (ysum[i, :, y] + yb_recv[i, 0]) + (yb_recv[i, 1] + yb_recv[i, 2])

    lax.fori_loop(4, 20, make_e, 0)

    for way in range(2):
        wait_bytes(precv.at[way, :PIECE], psem.at[way])
    for way in range(2):
        for k in (2, 1, 3):
            send(
                precv.at[way, pl.ds(piece_row, PIECE)],
                precv.at[way, pl.ds(piece_row, PIECE)],
                sent.at[7], fsem.at[0], band_of(x_lo, y_at(k), core), space,
            )
    make_item(0)
    make_item(1)
    make_item(2)
    lax.fori_loop(0, 4, make_e, 0)
    lax.fori_loop(20, 24, make_e, 0)
    wait_bytes(precv.at[0, : 6 * PIECE], fsem.at[0])
    core_row = pl.multiple_of(core * 4 * PIECE, 8)
    for way in range(2):
        send(
            precv.at[way, pl.ds(core_row, 4 * PIECE)],
            precv.at[way, pl.ds(core_row, 4 * PIECE)],
            sent.at[8], fsem.at[1], band_of(x_lo, y, 1 - core), space,
        )
    ya_start(0)
    ya_start(1)
    ya_start(2)

    def take_halo(chunk):
        start, count, places = CHUNKS[chunk]
        half = count // 2
        for way in range(2):
            wait_bytes(orecv.at[way, :, start : start + count + half], osem.at[way, chunk])
            for layer in range(4):
                main = orecv[way, layer, start : start + count]
                tail = orecv[way, layer, start + count : start + count + half]
                row = layer * ROWS + start
                unpack_into(orb_halo, (4 * way + layer,), chunk, main, tail)
                main = main * precv[way, row : row + count]
                tail = tail * precv[way, row + count : row + count + half]
                unpack_into(v_halo, (4 * way + layer,), chunk, main, tail)
        for _, row, size in places:
            rows = slice(row, row + size)
            for x in range(4):
                below = WEIGHTS[3] * v_halo[x, rows]
                for layer in range(x + 1, 4):
                    below += WEIGHTS[3 + x - layer] * v_halo[layer, rows]
                e[x + 8, rows] += b_sten * below
                above = WEIGHTS[3] * v_halo[4 + x, rows]
                for layer in range(x):
                    above += WEIGHTS[3 + layer - x] * v_halo[4 + layer, rows]
                e[x + 28, rows] += b_sten * above

    wait_bytes(precv.at[0, : 8 * PIECE], fsem.at[1])
    take_halo(0)
    make_item(3)
    make_item(4)
    ya_start(3)
    make_item(5)
    ya_start(4)
    ya_start(5)
    for n in range(0, 3):
        ya_end(n)
    take_halo(1)
    make_item(6)
    make_item(7)
    ya_start(6)
    make_item(8)
    ya_start(7)
    ya_start(8)
    prepare(10)
    for n in range(3, 6):
        ya_end(n)
    take_halo(2)
    make_item(9)
    make_item(11)
    xa_start(9)
    make_item(10)
    xa_start(11)
    ya_start(10)
    for n in range(6, 9):
        ya_end(n)
    xa_end(9)
    for n in range(0, 6):
        xb_end(n)

    mine_at = core * 8 + space

    def to_columns(side):
        blocks = slice(2 * side, 2 * side + 2)
        value = jnp.concatenate(
            [red[chunk, blocks].reshape(96, 128) for chunk in range(3)], axis=1
        )
        high, low = split(value)
        for layer in range(2):
            table_high, table_low = pair_of("forward_y%d" % layer)
            columns = dot(high, table_high) + (dot(low, table_high) + dot(high, table_low))
            for j in range(4):
                for half in range(2):
                    gsend[side, pl.ds(half * 8 + 2 * j + layer, 24, stride=16), :] = columns[
                        24 * j : 24 * j + 24, 128 * half : 128 * half + 128
                    ]
        for k in (3, 5, 1, 7, 4, 2, 6, 0):
            for c in range(2):
                if (k, c) != (0, 0):
                    to_space = lax.rem(space + k, 8)
                    to_core = lax.rem(core + c, 2)
                    row = pl.multiple_of(24 * (to_core * 8 + to_space), 8)
                    send(
                        gsend.at[side, pl.ds(row, 24)], grecv.at[side, mine_at],
                        gsem.at[2], gsem.at[side], band_of(x_lo, y, to_core), to_space,
                    )
        grecv[side, mine_at] = gsend[side, pl.ds(pl.multiple_of(24 * mine_at, 8), 24), :]

    ya_end(10)
    xa_end(11)
    for n in (6, 7, 8, 10):
        xb_end(n)
    to_columns(0)
    yb_end(9)
    yb_end(11)
    to_columns(1)

    kx = lax.broadcasted_iota(jnp.int32, (NG, 128), 0)
    lane = lax.broadcasted_iota(jnp.int32, (NG, 128), 1)
    gx = jnp.minimum(kx, NG - kx)
    factors = []
    for unit in range(3):
        number = 3 * mine_at + unit
        kz = 24 * group + number // 2
        gz = jnp.minimum(kz, NG - kz)
        ky = lane + 128 * lax.rem(number, 2)
        gy = jnp.minimum(ky, NG - ky)
        square = (gx * gx + gy * gy + (gz * gz + 1)).astype(F32)
        factors.append((256.0 / float(NG) ** 3) / jnp.sqrt(square))
    coulomb = jnp.concatenate(factors, axis=1)

    for side in range(2):
        wait_bytes(grecv.at[side, :15], gsem.at[side])
    pencil = jnp.concatenate(
        [grecv[:, :, 8 * unit : 8 * unit + 8, :].reshape(256, 128) for unit in range(3)], axis=1
    )
    spectral = dot3_table_left(pair_of("forward_x"), pencil) * coulomb
    restored = dot3_table_left(pair_of("plain"), spectral)
    for unit in range(3):
        wsend[unit] = restored[:, 128 * unit : 128 * unit + 128]

    for third in range(3):
        for k in (3, 5, 1, 7, 4, 2, 6):
            to_space = lax.rem(space + k, 8)
            row = pl.multiple_of(24 * to_space + 8 * third, 8)
            send(
                wsend.at[:, pl.ds(row, 8)], wrecv.at[third, pl.ds(3 * space, 3)],
                wsem.at[3], wsem.at[third], band, to_space,
            )
    for third in range(3):
        own_row = pl.multiple_of(24 * space + 8 * third, 8)
        wrecv[third, pl.ds(3 * space, 3)] = wsend[:, pl.ds(own_row, 8), :]
    brow[...] = jnp.zeros(brow.shape, F32)
    for third in range(3):
        wait_bytes(wrecv.at[third, :21], wsem.at[third])
        for unit in range(24):
            brow[unit % 2, pl.ds(128 * third + unit // 2, 8, stride=16), :] = wrecv[third, unit]
        rows = jnp.concatenate(
            [brow[half, 128 * third : 128 * third + 128] for half in range(2)], axis=1
        )
        zsend[third] = dot3_table_left(pair_of("inverse_y"), rows, ((1,), (1,))).reshape(48, 4, 128)
        for k in (4, 12, 8, 3, 5, 11, 13, 2, 6, 10, 14, 7, 9, 1, 15):
            to = lax.rem(band + k, 16)
            send(
                zsend.at[third, pl.ds(3 * to, 3)], zrecv.at[third, band],
                zsem.at[3], zsem.at[third], to, space,
            )
        zrecv[third, band] = zsend[third, pl.ds(3 * band, 3)]

    granule = lax.broadcasted_iota(jnp.int32, (12, 128), 1) // 16
    for third in range(3):
        wait_bytes(zrecv.at[third, :15], zsem.at[third])
        for side in range(2):
            blocks = [zrecv[third, 8 * side + i].reshape(12, 128) for i in range(8)]
            for bit in (1, 2, 4):
                upper = lax.rem(granule // bit, 2) == 1
                after = list(blocks)
                for i in range(8):
                    if not i & bit:
                        low, high = blocks[i], blocks[i | bit]
                        after[i] = jnp.where(upper, pltpu.roll(high, 16 * bit, 1), low)
                        after[i | bit] = jnp.where(upper, high, pltpu.roll(low, 128 - 16 * bit, 1))
                blocks = after
            for i in range(8):
                mat[side, pl.ds(i, 12, stride=8), :] = blocks[i]
        rows = jnp.concatenate([mat[0], mat[1]], axis=1)
        result = dot3_table_right(rows, pair_of("inverse_z"))
        out[0, :, 8 * third : 8 * third + 8] = result.reshape(12, 8, NG)

    wait_bytes(psend.at[:, :PIECE], sent.at[0])
    wait_bytes(osend, sent.at[1])
    wait_bytes(other, sent.at[2])
    wait_bytes(ya_recv, sent.at[3])
    wait_bytes(xb_recv, sent.at[4])
    wait_bytes(xa_recv, sent.at[5])
    wait_bytes(yb_recv, sent.at[6])
    wait_bytes(precv.at[0, : 6 * PIECE], sent.at[7])
    wait_bytes(precv.at[0, : 8 * PIECE], sent.at[8])
    wait_bytes(grecv.at[:, :15], gsem.at[2])
    wait_bytes(wrecv.at[:, :21], wsem.at[3])
    wait_bytes(zrecv.at[:, :15], zsem.at[3])


def on_device(orbitals, occupations, shifts, perturbations, local_potential):
    any_space = pl.BlockSpec(memory_space=pl.ANY)
    smem = pl.BlockSpec(memory_space=pltpu.SMEM)
    vmem = pl.BlockSpec(memory_space=pltpu.VMEM)
    dma = pltpu.SemaphoreType.DMA
    response = pl.pallas_call(
        kernel,
        out_shape=jax.ShapeDtypeStruct((1, 12, SLAB, NG), F32),
        in_specs=[smem] * 2 + [any_space] * 4,
        out_specs=vmem,
        scratch_shapes=[
            pltpu.VMEM(TABLE.shape, BF16),
            pltpu.VMEM((EXT, NG, NG), BF16),
            pltpu.VMEM((EXT, NG, NG), F32),
            pltpu.VMEM((SLAB, NG, NG), F32),
            pltpu.VMEM((EXT, NG, NG), F32),
            pltpu.VMEM((EXT + 8, NG, NG), F32),
            pltpu.VMEM((2, 4, ROWS, 128), F32),
            pltpu.VMEM((2, 4, ROWS, 128), F32),
            pltpu.VMEM((2, ROWS, 128), F32),
            pltpu.VMEM((2, 4 * ROWS, 128), F32),
            pltpu.VMEM((8, NG, NG), F32),
            pltpu.VMEM((8, NG, NG), F32),
            pltpu.VMEM((12, 4, 64, NG), F32),
            pltpu.VMEM((12, 4, 64, NG), F32),
            pltpu.VMEM((12, 4, 64, NG), F32),
            pltpu.VMEM((12, 2, 4, 2, 24, 128), F32),
            pltpu.VMEM((10, 3, 2, 2, 24, 128), F32),
            pltpu.VMEM((10, 2, 2, 24, 128), F32),
            pltpu.VMEM((10, 2, 24, 128), F32),
            pltpu.VMEM((2, 2, 4, 24, 128), F32),
            pltpu.VMEM((2, 2, 4, 24, 128), F32),
            pltpu.VMEM((2, 3, 2, 24, 128), F32),
            pltpu.VMEM((3, 4, 2, 24, 128), F32),
            pltpu.VMEM((2, 4, 64, NG), F32),
            pltpu.VMEM((2, 384, 128), F32),
            pltpu.VMEM((2, 16, 24, 128), F32),
            pltpu.VMEM((3, NG, 128), F32),
            pltpu.VMEM((3, 24, 8, 128), F32),
            pltpu.VMEM((2, 384, 128), F32),
            pltpu.VMEM((3, 48, 4, 128), F32),
            pltpu.VMEM((3, 16, 3, 4, 128), F32),
            pltpu.VMEM((2, 96, 128), F32),
            dma((8,)),
            dma((2, 3)),
            dma((2,)),
            dma((2,)),
            dma((12,)),
            dma((10,)),
            dma((10,)),
            dma((2,)),
            dma((2,)),
            dma((3,)),
            dma((4,)),
            dma((4,)),
            dma((9,)),
        ],
        compiler_params=pltpu.CompilerParams(
            collective_id=0, has_side_effects=True, vmem_limit_bytes=60 * 2**20
        ),
        name="response",
    )(occupations, shifts, orbitals, perturbations, local_potential, jnp.asarray(TABLE))
    return jnp.transpose(response, (0, 2, 1, 3))


def solution(mesh):
    in_specs = (
        P("band", "space", None, None),
        P("band"),
        P("band"),
        P(None, "space", None, None),
        P("space", None, None),
    )
    out_specs = P(None, "space", "band", None)
    return jax.shard_map(
        on_device, mesh=mesh, in_specs=in_specs, out_specs=out_specs, check_vma=False
    )
```
